256 devices in a mesh: row: 32 (over z, y), col: 8 (over x, core).
Axes of the slice: x: 4, y: 4, z: 8, core: 2. Of those that a mesh axis runs over, the one named last changes fastest.
Arguments:
- acts: bfloat16 [2048, 8192], P('col', 'row'), may hold values from -6 to 6
- output_cotangent: bfloat16 [2048, 28672], P('row', 'col'), may hold values from -0.29882812 to 0.29882812
- frozen: bfloat16 [8192, 28672], P('row', 'col'), may hold values from -0.0625 to 0.0625
- down_factors: float32 [4, 16, 28672], P(None, None, 'col'), may hold values from -0.10630251 to 0.10630251
- up_factors: float32 [4, 8192, 16], P(None, 'row'), may hold values from -0.19887379 to 0.19887379
- magnitude: float32 [4, 28672], P(None, 'col'), may hold values from 0.5 to 2
- slot_trial_index: int32 [16], replicated, may hold values from 0 to 3, as said below
Outputs:
- activation_gradient: bfloat16 [2048, 8192], P('col', 'row')
- magnitude_gradient: float32 [4, 28672], P(None, 'col')
- down_factor_gradient: float32 [4, 16, 28672], P(None, None, 'col')
- up_factor_gradient: float32 [4, 8192, 16], P(None, 'row')
The draws below stay inside these ranges and needn't reach their ends.
Inputs may be any that keep to these rules, and one draw needn't show every extreme that they name: `slot_trial_index`: each of the 4 trials is named by exactly 4 slots.
All inputs are finite; a program needn't handle non-finite values.
Results may differ from the reference program's by a relative error of at most 0.0049.
Values may be sent and summed in bfloat16 or wider, within the bound.
A program may use at most 192 MiB of HBM per device.

```python
import math
import jax
import jax.numpy as jnp
from jax import lax

MODEL_WIDTH = 8192
HIDDEN_UNITS = 28672
ADAPTER_RANK = 16
TRIAL_COUNT = 4
SLOTS = 16
TOKENS = 2048


def draw_slot_trial_index(key, part):
    key = jax.random.fold_in(key, 7)
    order = jax.random.permutation(key, SLOTS)
    return (order % TRIAL_COUNT).astype(jnp.int32)


def block_levels(own_key, shape, cuts, least, top_value):
    def one(axis_at, parts):
        draws = jax.random.uniform(jax.random.fold_in(jax.random.fold_in(own_key, 6), axis_at), (parts,), jnp.float32, least / len(cuts), top_value / len(cuts))
        return jnp.repeat(jnp.exp(draws), shape[axis_at] // parts).reshape((-1,) + (1,) * (len(shape) - axis_at - 1))

    level = one(*cuts[0])
    for cut in cuts[1:]:
        level = level * one(*cut)
    return level


def centred(stream_key, shape, width, reach, pieces=(), kind=jnp.bfloat16):
    entries = width * jax.random.normal(stream_key, shape, jnp.float32)
    if pieces:
        entries = entries * block_levels(stream_key, shape, pieces, -0.22, 0.18)
    return jnp.clip(entries, -reach, reach).astype(kind)


def setup_inputs(seed: int = 0) -> dict:
    splits = jax.random.split(jax.random.key(seed), 8)
    acts = centred(splits[0], (TOKENS, MODEL_WIDTH), 1.0, 6.0, ((0, 8), (1, 32)))
    output_cotangent = centred(splits[1], (TOKENS, HIDDEN_UNITS), 0.05, 0.29882812, ((0, 32), (1, 8)))
    frozen = centred(splits[2], (MODEL_WIDTH, HIDDEN_UNITS), MODEL_WIDTH ** -0.5, 0.0625, ((0, 32), (1, 8)))
    down_factors = centred(splits[3], (TRIAL_COUNT, ADAPTER_RANK, HIDDEN_UNITS), (3.0 / HIDDEN_UNITS ** 0.5), 0.10630251, ((2, 8),), jnp.float32)
    up_factors = centred(splits[4], (TRIAL_COUNT, MODEL_WIDTH, ADAPTER_RANK), (3.0 / MODEL_WIDTH ** 0.5), 0.19887379, ((1, 32),), jnp.float32)
    magnitude = jnp.clip(jnp.exp(math.log(2.0) - 1.3862944 * jax.random.uniform(splits[5], (TRIAL_COUNT, HIDDEN_UNITS), jnp.float32) ** block_levels(splits[5], (TRIAL_COUNT, HIDDEN_UNITS), ((1, 8),), -0.2, 0.2)), 0.5, 2.0)
    slot_trial_index = draw_slot_trial_index(jax.random.fold_in(splits[7], 71), 0)
    return {"acts": acts, "output_cotangent": output_cotangent, "frozen": frozen, "down_factors": down_factors, "up_factors": up_factors, "magnitude": magnitude, "slot_trial_index": slot_trial_index}


ADAPTER_SCALE = 2.0
EPS = 1e-06
HIGH_PRECISION = lax.Precision.HIGHEST

def reference(acts, output_cotangent, frozen, down_factors, up_factors, magnitude, slot_trial_index):
    tokens = acts.shape[0]
    slot_len = tokens // SLOTS
    owner_ids = jnp.repeat(slot_trial_index, slot_len, total_repeat_length=tokens)
    owner = (owner_ids[:, None] == jnp.arange(TRIAL_COUNT, dtype=jnp.int32)[None, :]).astype(jnp.float32)
    spread = jnp.repeat(owner, ADAPTER_RANK, axis=1)
    column_block = 512 if HIDDEN_UNITS % 512 == 0 else HIDDEN_UNITS
    count = HIDDEN_UNITS // column_block

    def col_block(index):
        block_start = (index * column_block).astype(jnp.int32)
        weight_columns = lax.dynamic_slice_in_dim(frozen, block_start, column_block, 1).astype(jnp.float32)
        factor_columns = lax.dynamic_slice_in_dim(down_factors, block_start, column_block, 2)
        merged_weight = weight_columns[None] + ADAPTER_SCALE * jnp.einsum('qby,qyi->qbi', up_factors, factor_columns, precision=HIGH_PRECISION)
        sums = lax.optimization_barrier(jnp.sum(merged_weight * merged_weight, axis=1))
        key_piece = jnp.einsum('qfh,qfp->qhp', up_factors, merged_weight, precision=HIGH_PRECISION)
        return (sums, key_piece)
    sums, kparts = lax.map(col_block, jnp.arange(count, dtype=jnp.int32))
    normsq = jnp.transpose(sums, (1, 0, 2)).reshape(TRIAL_COUNT, HIDDEN_UNITS)
    key_matrix_term = jnp.transpose(kparts, (1, 2, 0, 3)).reshape(TRIAL_COUNT, ADAPTER_RANK, HIDDEN_UNITS)
    col_norm = jnp.sqrt(normsq + EPS)
    rescale_factor = magnitude / col_norm
    xfull = acts.astype(jnp.float32)
    stacked_up_factors = jnp.transpose(up_factors, (1, 0, 2)).reshape(MODEL_WIDTH, TRIAL_COUNT * ADAPTER_RANK)
    stacked_down_factors = down_factors.reshape(TRIAL_COUNT * ADAPTER_RANK, HIDDEN_UNITS)
    qmat = jnp.dot(xfull, stacked_up_factors, precision=HIGH_PRECISION) * spread
    pre = jnp.dot(acts, frozen, preferred_element_type=jnp.float32) + ADAPTER_SCALE * jnp.dot(qmat, stacked_down_factors, precision=HIGH_PRECISION)
    dyf = output_cotangent.astype(jnp.float32)
    dscale = jnp.dot(owner.T, dyf * pre, precision=HIGH_PRECISION)
    magnitude_gradient = dscale / col_norm
    grad_pre = (dyf * jnp.dot(owner, rescale_factor, precision=HIGH_PRECISION)).astype(jnp.bfloat16)
    gradient_factor = -dscale * magnitude / (col_norm * col_norm * col_norm)
    pmat = jnp.dot(grad_pre.astype(jnp.float32), stacked_down_factors.T, precision=HIGH_PRECISION) * spread
    activation_gradient = (jnp.dot(grad_pre, frozen.T, preferred_element_type=jnp.float32) + ADAPTER_SCALE * jnp.dot(pmat, stacked_up_factors.T, precision=HIGH_PRECISION)).astype(jnp.bfloat16)
    query_cotangent = jnp.dot(qmat.T, dyf, precision=HIGH_PRECISION).reshape(TRIAL_COUNT, ADAPTER_RANK, HIDDEN_UNITS)
    down_factor_gradient = ADAPTER_SCALE * (query_cotangent * rescale_factor[:, None, :] + key_matrix_term * gradient_factor[:, None, :])
    scaled_down_factor = (down_factors * gradient_factor[:, None, :]).reshape(TRIAL_COUNT * ADAPTER_RANK, HIDDEN_UNITS)

    def wag_step(carry, index):
        block_start = (index * column_block).astype(jnp.int32)
        weight_columns = lax.dynamic_slice_in_dim(frozen, block_start, column_block, 1).astype(jnp.float32)
        factor_columns = lax.dynamic_slice_in_dim(scaled_down_factor, block_start, column_block, 1)
        return (carry + jnp.dot(weight_columns, factor_columns.T, precision=HIGH_PRECISION), None)
    weight_gradient_step, unused = lax.scan(wag_step, jnp.zeros((MODEL_WIDTH, TRIAL_COUNT * ADAPTER_RANK), jnp.float32), jnp.arange(count, dtype=jnp.int32))
    inner_product = jnp.einsum('bzg,big->bzi', down_factors * gradient_factor[:, None, :], down_factors, precision=HIGH_PRECISION)
    up_factor_magnitude = jnp.einsum('qmo,qor->qmr', up_factors, inner_product, precision=HIGH_PRECISION)
    input_piece = jnp.dot(xfull.T, pmat, precision=HIGH_PRECISION)
    up_factor_gradient = ADAPTER_SCALE * (jnp.transpose((input_piece + weight_gradient_step).reshape(MODEL_WIDTH, TRIAL_COUNT, ADAPTER_RANK), (1, 0, 2)) + ADAPTER_SCALE * up_factor_magnitude)
    return (activation_gradient, magnitude_gradient, down_factor_gradient, up_factor_gradient)
```

```python
import functools

import jax
import jax.numpy as jnp
from jax import lax
from jax.experimental import pallas as pl
from jax.experimental.pallas import tpu as pltpu
from jax.sharding import PartitionSpec as P

SCALE = 2.0
EPS = 1e-06
NX, NY, NZ = 4, 4, 8
MESH = pl.DeviceIdType.MESH
F32, BF16 = jnp.float32, jnp.bfloat16
RP = 128


def mm(a, b, ca, cb, precision=None):
    return lax.dot_general(
        a, b, (((ca,), (cb,)), ((), ())), precision=precision, preferred_element_type=F32
    )


def kernel(
    acts, dy, w, dn, ut, mag, idx,
    out_dx, out_mag, out_dn, out_up,
    dyA, X, Wg, Wo, Ug, Uo, UTs, Df, Dq, Db,
    nyS, nyR, nzS, nzR, resS,
    dsS, dsR, gfS, qacc, kacc, xpT, qkS, qkR,
    dxo, dxs, pairR, xs, xR, ysS, ysR,
    upS, upR, upP, upPR, upX, upXR, mgR, dnQ,
    ss, rs, ls, ps, pr, xss, xrs,
):
    row, col = lax.axis_index("row"), lax.axis_index("col")
    z, y = lax.div(row, NY), lax.rem(row, NY)
    x, k = lax.div(col, 2), lax.rem(col, 2)
    rank = 16
    trials = 4
    rows = dy.shape[0]
    cols = w.shape[1]
    qc = cols // NY
    wd = w.shape[0]
    tok = acts.shape[0]

    def mod(v, n):
        return lax.rem(v + n, n)

    def at_y(j):
        return (z * NY + mod(y + j, NY), col)

    def at_z(j):
        return (mod(z + j, NZ) * NY + y, col)

    def at_x(j):
        return (row, mod(x + j, NX) * 2 + k)

    sib = (row, x * 2 + 1 - k)
    YJ, XJ = (1, 3, 2), (1, 3, 2)

    barrier = pltpu.get_barrier_semaphore()
    peers = [at_y(j) for j in YJ] + [at_x(j) for j in XJ] + [at_z(j) for j in range(1, NZ)] + [sib]
    for p in peers:
        pl.semaphore_signal(barrier, inc=1, device_id=p, device_id_type=MESH)
    pl.semaphore_wait(barrier, len(peers))

    count = [0, 0]
    sent = []

    def remote(src, dst, dev, start=True):
        i = count[0]
        count[0] += 1
        d = pltpu.make_async_remote_copy(
            src_ref=src, dst_ref=dst, send_sem=ss.at[i], recv_sem=rs.at[i],
            device_id=dev, device_id_type=MESH,
        )
        if start:
            d.start()
        sent.append(d)
        return d

    def localcp(src, dst):
        i = count[1]
        count[1] += 1
        d = pltpu.make_async_copy(src, dst, ls.at[i])
        d.start()
        return d

    def yq(j):
        return pl.ds(pl.multiple_of(mod(y + j, NY) * qc, 128), qc)

    yrows = pl.ds(pl.multiple_of(y * rows, rows), rows)
    ywd = pl.ds(pl.multiple_of(y * wd, wd), wd)

    dy_local = localcp(dy.at[:, yq(0)], dyA.at[z, yrows, :])
    dy_y = [remote(dy.at[:, yq(j)], dyA.at[z, yrows, :], at_y(j)) for j in YJ]
    ut_local = localcp(ut, UTs.at[pl.ds(0, trials * rank), :])
    act_local = localcp(acts, X.at[col, :, ywd])
    act_y = [remote(acts, X.at[col, :, ywd], at_y(j)) for j in YJ]
    df_local = localcp(dn, Df.at[pl.ds(0, trials * rank), :])
    wo_local = localcp(w, Wo)
    UTs[trials * rank :, :] = jnp.zeros((RP - trials * rank, wd), F32)
    Df[trials * rank :, :] = jnp.zeros((RP - trials * rank, cols), F32)
    ut_local.wait()
    Uo[...] = UTs[...].T.astype(BF16)
    u_local = localcp(Uo, Ug.at[ywd, :])
    u_y = [remote(Uo, Ug.at[ywd, :], at_y(j)) for j in YJ]
    wg_local = localcp(w.at[:, yq(0)], Wg.at[ywd, :])
    w_y = [remote(w.at[:, yq(j)], Wg.at[ywd, :], at_y(j)) for j in YJ]

    ring = {}

    def zsend(sign, step, b):
        ys = mod(y - (0, 1, 3, 2)[b], NY)
        src = dyA.at[
            mod(z - sign * (step - 1), NZ), pl.ds(pl.multiple_of(ys * rows, rows), rows), :
        ]
        ring[sign, step, b] = remote(src, src, at_z(sign))

    def zstep(step, b):
        for sign in (1, -1):
            if step > 1:
                ring[sign, step - 1, b].wait_recv()
            if step < 4 or (b < 2) == (sign == 1):
                zsend(sign, step, b)

    dy_local.wait()
    zstep(1, 0)
    for b, d in enumerate(dy_y):
        d.wait_recv()
        zstep(1, b + 1)

    df_local.wait()
    wo_local.wait()
    nyS[...] = jnp.zeros_like(nyS)
    half = qc // 2

    def norm_piece(yy):
        for h in range(2):
            c0 = yy * qc + h * half
            wb = Wo[:, c0 : c0 + half].astype(F32)
            db = (SCALE * Df[:, c0 : c0 + half]).astype(BF16)
            owner = lax.broadcasted_iota(jnp.int32, db.shape, 0) // rank
            for t in range(trials):
                m = wb + mm(Uo[...], jnp.where(owner == t, db, jnp.zeros_like(db)), 1, 0)
                nyS[yy, t : t + 1, h * half : (h + 1) * half] = jnp.sum(m * m, axis=0, keepdims=True)

    for yy in range(NY):
        norm_piece(yy)
        zstep(2, yy)
    ny_y = [remote(nyS.at[mod(y + j, NY)], nyR.at[y], at_y(j)) for j in YJ]
    zstep(3, 0)
    act_local.wait()
    for d in act_y:
        d.wait_recv()
    x_x = [remote(X.at[col], X.at[col], at_x(j)) for j in XJ]
    x_sib = [remote(X.at[col], X.at[col], sib)]
    zstep(3, 1)
    for d in ny_y:
        d.wait_recv()
    nzS[...] = (
        nyS[y] + nyR[mod(y + 1, NY)] + nyR[mod(y + 2, NY)] + nyR[mod(y + 3, NY)]
    )
    nz_z = [remote(nzS, nzR.at[z], at_z(j)) for j in range(1, NZ)]
    zstep(3, 2)
    zstep(3, 3)
    dq_load = Df[:, pl.ds(pl.multiple_of(y * qc, 128), qc)]
    Dq[...] = dq_load
    Db[...] = dq_load.astype(BF16)
    for b in range(NY):
        zstep(4, b)
    for j, d in zip(XJ, x_x):
        d.wait_recv()
        src = X.at[mod(x - j, NX) * 2 + k]
        x_sib.append(remote(src, src, sib))
    u_local.wait()
    wg_local.wait()
    for d in u_y + w_y:
        d.wait_recv()

    same = (
        lax.broadcasted_iota(jnp.int32, (RP, RP), 0) // rank
        == lax.broadcasted_iota(jnp.int32, (RP, RP), 1) // rank
    )
    gram = jnp.where(same, mm(Ug[...], Ug[...], 0, 0), 0.0)
    kacc[...] = mm(Ug[...], Wg[...], 0, 0) + SCALE * mm(gram.astype(BF16), Db[...], 1, 0)

    for d in nz_z:
        d.wait_recv()
    nsq = nzS[...]
    for j in range(1, NZ):
        nsq = nsq + nzR[mod(z + j, NZ)]
    norm = jnp.sqrt(nsq[:trials] + EPS)
    magq = mag[:, pl.ds(pl.multiple_of(y * qc, 128), qc)]
    resS[0:trials, :] = magq / norm

    for d in x_sib:
        d.wait_recv()
    for key in ((1, 4, 0), (1, 4, 1), (-1, 4, 2), (-1, 4, 3)):
        ring[key].wait_recv()

    dsS[...] = jnp.zeros_like(dsS)
    qacc[...] = jnp.zeros_like(qacc)
    xpT[...] = jnp.zeros_like(xpT)
    hrow = tok // 2

    def chunk_of(i):
        s = lax.div(i + 1, 2)
        return lax.rem(z + s * (2 * lax.rem(i, 2) - 1) + NZ, NZ)

    def pair_copy(slot):
        return pltpu.make_async_remote_copy(
            src_ref=dxs.at[slot], dst_ref=pairR.at[slot], send_sem=ps.at[slot],
            recv_sem=pr.at[slot], device_id=sib, device_id_type=MESH,
        )

    def x_copy(to, frm):
        return pltpu.make_async_remote_copy(
            src_ref=xs.at[to], dst_ref=xR.at[frm], send_sem=xss.at[to],
            recv_sem=xrs.at[frm], device_id=(row, to * 2 + k), device_id_type=MESH,
        )

    def compute(i):
        c = chunk_of(i)
        xc = X[c]
        dyc = dyA[c]
        t0, t1 = idx[2 * c], idx[2 * c + 1]
        sub = lax.broadcasted_iota(jnp.int32, (tok, RP), 0)
        lane = lax.broadcasted_iota(jnp.int32, (tok, RP), 1)
        mask = lane // rank == jnp.where(sub < hrow, t0, t1)
        q = jnp.where(mask, mm(xc, Ug[...], 1, 0), 0.0).astype(BF16)
        pre = mm(xc, Wg[...], 1, 0) + SCALE * mm(q, Db[...], 1, 0)
        dyf = dyc.astype(F32)
        e = dyf * pre
        trow = lax.broadcasted_iota(jnp.int32, (8, qc), 0)
        s0 = jnp.sum(e[:hrow], axis=0, keepdims=True)
        s1 = jnp.sum(e[hrow:], axis=0, keepdims=True)
        dsS[...] += jnp.where(trow == t0, s0, 0.0) + jnp.where(trow == t1, s1, 0.0)
        res = resS[0:trials, :]
        r0 = jnp.zeros((1, qc), F32)
        r1 = jnp.zeros((1, qc), F32)
        for t in range(trials):
            r0 = jnp.where(t0 == t, res[t : t + 1], r0)
            r1 = jnp.where(t1 == t, res[t : t + 1], r1)
        gp = jnp.concatenate(
            [(dyf[:hrow] * r0).astype(BF16), (dyf[hrow:] * r1).astype(BF16)], axis=0
        )
        p = jnp.where(mask, mm(gp, Db[...], 1, 1), 0.0).astype(BF16)
        qacc[...] += mm(q, dyc, 0, 0)
        xpT[...] += mm(p, xc, 0, 0)
        dx = mm(gp, Wg[...], 1, 1) + SCALE * mm(p, Ug[...], 1, 1)
        slot = lax.div(c, 2)

        @pl.when(lax.rem(c, 2) == k)
        def _():
            dxo[slot] = dx

        @pl.when(lax.rem(c, 2) != k)
        def _():
            dxs[slot] = dx.astype(BF16)
            pair_copy(slot).start()

    def pass_on(i):
        c = chunk_of(i)
        slot = lax.div(c, 2)

        @pl.when(lax.rem(c, 2) == k)
        def _():
            pair_copy(slot).wait_recv()
            total = dxo[slot] + pairR[slot].astype(F32)

            @pl.when(slot == x)
            def _():
                dxo[slot] = total

            @pl.when(slot != x)
            def _():
                xs[slot] = total.astype(BF16)
                x_copy(slot, x).start()

    def step(i, carry):
        compute(i)

        @pl.when(i > 0)
        def _():
            pass_on(i - 1)

        return carry

    lax.fori_loop(0, NZ, step, 0)

    ds_z = [remote(dsS, dsR.at[z], at_z(j)) for j in range(1, NZ)]
    for zz in range(NZ):
        qkS[zz, 0:8, :] = qacc[8 * zz : 8 * zz + 8, :]
        qkS[zz, 8:16, :] = kacc[8 * zz : 8 * zz + 8, :]
    qk_z = [remote(qkS.at[mod(z + j, NZ)], qkR.at[z], at_z(j)) for j in range(1, NZ)]
    pass_on(NZ - 1)
    for d in ds_z:
        d.wait_recv()
    dsum = dsS[...]
    for j in range(1, NZ):
        dsum = dsum + dsR[mod(z + j, NZ)]
    dsum = dsum[:trials]
    mgR[y, 0:trials, :] = dsum / norm
    mg_y = [remote(mgR.at[y], mgR.at[y], at_y(j)) for j in YJ]
    gf = -dsum * magq / (norm * norm * norm)
    gfS[0:trials, :] = gf
    dg = jnp.concatenate(
        [Dq[rank * t : rank * (t + 1), :] * gf[t : t + 1] for t in range(trials)]
        + [jnp.zeros((RP - trials * rank, qc), F32)],
        axis=0,
    ).astype(BF16)
    inner = jnp.where(same, mm(dg, Db[...], 1, 1), 0.0).astype(BF16)
    up = SCALE * (xpT[...] + mm(dg, Wg[...], 1, 1) + SCALE * mm(inner, Ug[...], 1, 1))
    for yy in range(NY):
        upS[yy] = up[: trials * rank, yy * wd : (yy + 1) * wd]
    up_y = [remote(upS.at[mod(y + j, NY)], upR.at[y], at_y(j)) for j in YJ]

    for d in qk_z:
        d.wait_recv()
    qk = qkS[z]
    for j in range(1, NZ):
        qk = qk + qkR[mod(z + j, NZ)]
    tz = lax.div(z * 8, rank)
    zrows = pl.ds(pl.multiple_of(z * 8, 8), 8)
    dnQ[zrows, :] = SCALE * (
        qk[0:8] * resS[pl.ds(tz, 1), :] + qk[8:16] * gfS[pl.ds(tz, 1), :]
    )
    dn_z = [remote(dnQ.at[zrows, :], dnQ.at[zrows, :], at_z(j)) for j in range(1, NZ)]

    for d in up_y:
        d.wait_recv()
    upP[...] = upS[y] + upR[mod(y + 1, NY)] + upR[mod(y + 2, NY)] + upR[mod(y + 3, NY)]
    up_p = remote(upP, upPR, sib)

    for d in dn_z:
        d.wait_recv()
    dn_local = localcp(dnQ, out_dn.at[:, yq(0)])
    dn_y = [remote(dnQ, out_dn.at[:, yq(0)], at_y(j)) for j in YJ]

    up_p.wait_recv()
    upX[...] = upP[...] + upPR[...]
    up_x = [remote(upX, upXR.at[x], at_x(j)) for j in XJ]

    for j in (1, 2, 3):
        x_copy(mod(x + j, NX), mod(x + j, NX)).wait_recv()
    total = dxo[x]
    for j in (1, 2, 3):
        total = total + xR[mod(x + j, NX)].astype(F32)
    dxo[x] = total
    for yy in range(NY):
        ysS[yy] = total[:, yy * wd : (yy + 1) * wd].astype(BF16)
    ys_y = [remote(ysS.at[mod(y + j, NY)], ysR.at[y], at_y(j)) for j in YJ]

    for d in up_x:
        d.wait_recv()
    out_up[...] = upX[...] + upXR[mod(x + 1, NX)] + upXR[mod(x + 2, NX)] + upXR[mod(x + 3, NX)]
    for d in mg_y:
        d.wait_recv()
    for yy in range(NY):
        out_mag[:, yy * qc : (yy + 1) * qc] = mgR[yy, 0:trials, :]
    for d in ys_y:
        d.wait_recv()
    acc = dxo[x, :, pl.ds(pl.multiple_of(y * wd, wd), wd)]
    for j in (1, 2, 3):
        acc = acc + ysR[mod(y + j, NY)].astype(F32)
    out_dx[...] = acc.astype(BF16)

    for d in dn_y:
        d.wait_recv()
    dn_local.wait()
    for d in sent:
        d.wait_send()
    for slot in range(4):
        pair_copy(slot).wait_send()
    for j in (1, 2, 3):
        x_copy(mod(x + j, NX), x).wait_send()


def local(acts, dy, w, down, up, mag, idx):
    trials, rank, cols = down.shape
    wd = w.shape[0]
    tok = acts.shape[0]
    qc = cols // NY
    tr = trials * rank
    dn = down.reshape(tr, cols)
    ut = jnp.transpose(up, (0, 2, 1)).reshape(tr, wd)
    V = pltpu.VMEM
    anyspec = pl.BlockSpec(memory_space=pl.ANY)
    vspec = pl.BlockSpec(memory_space=pltpu.VMEM)
    sspec = pl.BlockSpec(memory_space=pltpu.SMEM)
    width = NY * wd
    scratch = [
        V((NZ, tok, qc), BF16),
        V((2 * NX, tok, width), BF16),
        V((width, qc), BF16),
        V((wd, cols), BF16),
        V((width, RP), BF16),
        V((wd, RP), BF16),
        V((RP, wd), F32),
        V((RP, cols), F32),
        V((RP, qc), F32),
        V((RP, qc), BF16),
        V((NY, 8, qc), F32),
        V((NY, 8, qc), F32),
        V((8, qc), F32),
        V((NZ, 8, qc), F32),
        V((8, qc), F32),
        V((8, qc), F32),
        V((NZ, 8, qc), F32),
        V((8, qc), F32),
        V((RP, qc), F32),
        V((RP, qc), F32),
        V((RP, width), F32),
        V((NZ, 16, qc), F32),
        V((NZ, 16, qc), F32),
        V((NX, tok, width), F32),
        V((NX, tok, width), BF16),
        V((NX, tok, width), BF16),
        V((NX, tok, width), BF16),
        V((NX, tok, width), BF16),
        V((NY, tok, wd), BF16),
        V((NY, tok, wd), BF16),
        V((NY, tr, wd), F32),
        V((NY, tr, wd), F32),
        V((tr, wd), F32),
        V((tr, wd), F32),
        V((tr, wd), F32),
        V((NX, tr, wd), F32),
        V((NY, 8, qc), F32),
        V((tr, qc), F32),
        pltpu.SemaphoreType.DMA((112,)),
        pltpu.SemaphoreType.DMA((112,)),
        pltpu.SemaphoreType.DMA((16,)),
        pltpu.SemaphoreType.DMA((NX,)),
        pltpu.SemaphoreType.DMA((NX,)),
        pltpu.SemaphoreType.DMA((NX,)),
        pltpu.SemaphoreType.DMA((NX,)),
    ]
    dx, mg, dng, upg = pl.pallas_call(
        kernel,
        out_shape=(
            jax.ShapeDtypeStruct((tok, wd), BF16),
            jax.ShapeDtypeStruct((trials, cols), F32),
            jax.ShapeDtypeStruct((tr, cols), F32),
            jax.ShapeDtypeStruct((tr, wd), F32),
        ),
        in_specs=[anyspec, anyspec, anyspec, anyspec, anyspec, vspec, sspec],
        out_specs=(vspec, vspec, anyspec, vspec),
        scratch_shapes=scratch,
        compiler_params=pltpu.CompilerParams(
            collective_id=0, has_side_effects=True, vmem_limit_bytes=56 * 1024 * 1024
        ),
        cost_estimate=pl.CostEstimate(flops=8_000_000_000, bytes_accessed=8_000_000, transcendentals=0),
    )(acts, dy, w, dn, ut, mag, idx)
    return (
        dx,
        mg,
        dng.reshape(trials, rank, cols),
        jnp.transpose(upg.reshape(trials, rank, wd), (0, 2, 1)),
    )


def solution(mesh):
    in_specs = (
        P("col", "row"),
        P("row", "col"),
        P("row", "col"),
        P(None, None, "col"),
        P(None, "row", None),
        P(None, "col"),
        P(),
    )
    out_specs = (P("col", "row"), P(None, "col"), P(None, None, "col"), P(None, "row", None))
    return jax.shard_map(local, mesh=mesh, in_specs=in_specs, out_specs=out_specs, check_vma=False)
```

```python
import functools

import jax
import jax.numpy as jnp
from jax import lax
from jax.experimental import pallas as pl
from jax.experimental.pallas import tpu as pltpu
from jax.sharding import PartitionSpec as P

SCALE = 2.0
EPS = 1e-06
NX, NY, NZ = 4, 4, 8
MESH = pl.DeviceIdType.MESH
F32, BF16 = jnp.float32, jnp.bfloat16
HP = 512
RP = 128


def mm(a, b, ca, cb, precision=None):
    return lax.dot_general(
        a, b, (((ca,), (cb,)), ((), ())), precision=precision, preferred_element_type=F32
    )


def pack(ref, v):
    n = v.shape[0]
    ref[0:n, :] = v[:, :HP]
    ref[n : 2 * n, 0 : v.shape[1] - HP] = v[:, HP:]


def unpack(p, cols):
    n = p.shape[0] // 2
    return jnp.concatenate([p[:n], p[n:, : cols - HP]], axis=1)


def kernel(
    acts, dy, w, dn, ut, mag, idx,
    out_dx, out_mag, out_dn, out_up,
    dyA, X, Wg, Wo, Ug, Uo, UTs, Df, Dq, Db,
    nyS, nyR, nzS, nzR, resS,
    dsS, dsP, dsR, gfS, qacc, kacc, xpT, qS, qR, kS, kR,
    gpA, pA, dxo, dxs, pairR, xs, xR, ysS, ysR, yfS, yfR, x2S, x2R, acc1,
    upS, upR, upP, upPR, upX, upXR, mgR, dnY,
    ss, rs, ls, ps, pr, xss, xrs, yfs, yfr, x2s, x2r,
):
    row, col = lax.axis_index("row"), lax.axis_index("col")
    z, y = lax.div(row, NY), lax.rem(row, NY)
    x, k = lax.div(col, 2), lax.rem(col, 2)
    rank = 16
    trials = 4
    rows = dy.shape[0]
    cols = w.shape[1]
    qc = cols // NY
    wd = w.shape[0]
    tok = acts.shape[0]
    tr = trials * rank
    hrow = tok // 2

    def mod(v, n):
        return lax.rem(v + n, n)

    def at_y(j):
        return (z * NY + mod(y + j, NY), col)

    def at_z(j):
        return (mod(z + j, NZ) * NY + y, col)

    def at_x(j):
        return (row, mod(x + j, NX) * 2 + k)

    sib = (row, x * 2 + 1 - k)
    YJ = (1, 3, 2)

    barrier = pltpu.get_barrier_semaphore()
    peers = [at_y(j) for j in YJ] + [at_x(j) for j in YJ] + [at_z(j) for j in range(1, NZ)] + [sib]
    for p in peers:
        pl.semaphore_signal(barrier, inc=1, device_id=p, device_id_type=MESH)

    count = [0, 0]
    sent = []

    def remote(src, dst, dev):
        i = count[0]
        count[0] += 1
        d = pltpu.make_async_remote_copy(
            src_ref=src, dst_ref=dst, send_sem=ss.at[i], recv_sem=rs.at[i],
            device_id=dev, device_id_type=MESH,
        )
        d.start()
        sent.append(d)
        return d

    def localcp(src, dst):
        i = count[1]
        count[1] += 1
        d = pltpu.make_async_copy(src, dst, ls.at[i])
        d.start()
        return d

    def yq(j):
        return pl.ds(pl.multiple_of(mod(y + j, NY) * qc, 128), qc)

    yrows = pl.ds(pl.multiple_of(y * rows, rows), rows)
    ywd = pl.ds(pl.multiple_of(y * wd, wd), wd)

    dy_local = localcp(dy.at[:, yq(0)], dyA.at[z, yrows, :])
    ut_local = localcp(ut, UTs.at[pl.ds(0, tr), :])
    wo_local = localcp(w, Wo)
    df_local = localcp(dn, Df.at[pl.ds(0, tr), :])
    act_local = localcp(acts, X.at[col, :, ywd])
    wg_local = localcp(w.at[:, yq(0)], Wg.at[ywd, :])
    UTs[tr:, :] = jnp.zeros((RP - tr, wd), F32)
    Df[tr:, :] = jnp.zeros((RP - tr, cols), F32)
    for ref in (dsS, qacc, xpT):
        ref[...] = jnp.zeros_like(ref)
    pl.semaphore_wait(barrier, len(peers))

    dy_y = [remote(dy.at[:, yq(j)], dyA.at[z, yrows, :], at_y(j)) for j in YJ]
    dy_local.wait()

    def chunk_of(i):
        s = lax.div(i + 1, 2)
        return lax.rem(z + s * (2 * lax.rem(i, 2) - 1) + NZ, NZ)

    def pair_copy(slot):
        return pltpu.make_async_remote_copy(
            src_ref=dxs.at[slot], dst_ref=pairR.at[slot], send_sem=ps.at[slot],
            recv_sem=pr.at[slot], device_id=sib, device_id_type=MESH,
        )

    def x_copy(to, frm):
        return pltpu.make_async_remote_copy(
            src_ref=xs.at[to], dst_ref=xR.at[frm], send_sem=xss.at[to],
            recv_sem=xrs.at[frm], device_id=(row, to * 2 + k), device_id_type=MESH,
        )

    def yf_copy(slot, j):
        return pltpu.make_async_remote_copy(
            src_ref=yfS.at[slot, mod(y + j, NY)], dst_ref=yfR.at[slot, y],
            send_sem=yfs.at[slot, j - 1], recv_sem=yfr.at[slot, j - 1],
            device_id=at_y(j), device_id_type=MESH,
        )

    def x2_copy(to, frm):
        return pltpu.make_async_remote_copy(
            src_ref=x2S.at[to], dst_ref=x2R.at[frm], send_sem=x2s.at[to],
            recv_sem=x2r.at[frm], device_id=(row, to * 2 + k), device_id_type=MESH,
        )

    def trials_of(c):
        t0, t1 = idx[2 * c], idx[2 * c + 1]
        sub = lax.broadcasted_iota(jnp.int32, (tok, RP), 0)
        lane = lax.broadcasted_iota(jnp.int32, (tok, RP), 1)
        return t0, t1, lane // rank == jnp.where(sub < hrow, t0, t1)

    def prep(i, carry):
        c = chunk_of(i)
        t0, t1, mask = trials_of(c)
        dyf = dyA[c].astype(F32)
        res = resS[0:trials, :]
        r0 = jnp.zeros((1, qc), F32)
        r1 = jnp.zeros((1, qc), F32)
        for t in range(trials):
            r0 = jnp.where(t0 == t, res[t : t + 1], r0)
            r1 = jnp.where(t1 == t, res[t : t + 1], r1)
        gpA[c, 0:hrow, :] = (dyf[:hrow] * r0).astype(BF16)
        gpA[c, hrow:, :] = (dyf[hrow:] * r1).astype(BF16)
        pA[c] = jnp.where(mask, mm(gpA[c], Db[...], 1, 1), 0.0).astype(BF16)
        return carry

    ring = {}

    def zstep(step, b):
        ys = mod(y - (0, 1, 3, 2)[b], NY)
        brows = pl.ds(pl.multiple_of(ys * rows, rows), rows)
        for sign in (1, -1):
            if step > 1:
                ring[sign, step - 1, b].wait_recv()
            if step < 4 or (b < 2) == (sign == 1):
                src = dyA.at[mod(z - sign * (step - 1), NZ), brows, :]
                ring[sign, step, b] = remote(src, src, at_z(sign))

    zstep(1, 0)
    act_y = [remote(acts, X.at[col, :, ywd], at_y(j)) for j in YJ]
    ut_local.wait()
    Uo[...] = UTs[...].T.astype(BF16)
    u_local = localcp(Uo, Ug.at[ywd, :])
    df_local.wait()
    wo_local.wait()

    def norm_piece(yy):
        for h, (c0, n) in enumerate(((0, HP), (HP, qc - HP))):
            at = slice(yy * qc + c0, yy * qc + c0 + n)
            wb = Wo[:, at].astype(F32)
            db = (SCALE * Df[:, at]).astype(BF16)
            owner = lax.broadcasted_iota(jnp.int32, db.shape, 0) // rank
            for t in range(trials):
                m = wb + mm(Uo[...], jnp.where(owner == t, db, jnp.zeros_like(db)), 1, 0)
                r = h * trials + t
                nyS[yy, r : r + 1, 0:n] = jnp.sum(m * m, axis=0, keepdims=True)

    norm_piece(0)
    norm_piece(1)
    for b, d in enumerate(dy_y):
        d.wait_recv()
        zstep(1, b + 1)
    u_y = [remote(Uo, Ug.at[ywd, :], at_y(j)) for j in YJ]
    norm_piece(2)
    norm_piece(3)
    ny_y = [remote(nyS.at[mod(y + j, NY)], nyR.at[y], at_y(j)) for j in YJ]
    zstep(2, 0)
    zstep(2, 1)

    act_local.wait()
    for d in act_y:
        d.wait_recv()
    w_y = [remote(w.at[:, yq(j)], Wg.at[ywd, :], at_y(j)) for j in YJ]
    h0, h1 = pl.ds(0, hrow), pl.ds(hrow, hrow)

    def xpart(j, h):
        return X.at[mod(x + j, NX) * 2 + k, h, :]

    def xwhole(j):
        return X.at[mod(x + j, NX) * 2 + k]

    xp = [remote(xpart(0, h), xpart(0, h), at_x(1)) for h in (h0, h1)]
    xm = [remote(xpart(0, h), xpart(0, h), at_x(-1)) for h in (h1, h0)]
    x_sib = [remote(xwhole(0), xwhole(0), sib)]
    zstep(2, 2)
    for d in ny_y:
        d.wait_recv()
    nzS[...] = nyS[y] + nyR[mod(y + 1, NY)] + nyR[mod(y + 2, NY)] + nyR[mod(y + 3, NY)]
    nz_z = [remote(nzS, nzR.at[z], at_z(j)) for j in range(1, NZ)]
    zstep(2, 3)
    zstep(3, 0)
    zstep(3, 1)
    xp[0].wait_recv()
    xp.append(remote(xpart(-1, h0), xpart(-1, h0), at_x(1)))
    xm[0].wait_recv()
    xm.append(remote(xpart(1, h1), xpart(1, h1), at_x(-1)))
    Dq[...] = Df[:, pl.ds(pl.multiple_of(y * qc, 128), qc)]
    Db[...] = Dq[...].astype(BF16)
    zstep(3, 2)
    for d in nz_z:
        d.wait_recv()
    nsq = nzS[...]
    for j in range(1, NZ):
        nsq = nsq + nzR[mod(z + j, NZ)]
    norm = jnp.sqrt(unpack(nsq, qc) + EPS)
    magq = mag[:, pl.ds(pl.multiple_of(y * qc, 128), qc)]
    resS[0:trials, :] = magq / norm
    zstep(3, 3)
    xp[1].wait_recv()
    xm[1].wait_recv()
    x_sib += [remote(xwhole(j), xwhole(j), sib) for j in (-1, 1)]
    zstep(4, 0)
    lax.fori_loop(0, 5, prep, 0)
    zstep(4, 1)
    xp[2].wait_recv()
    xm[2].wait_recv()
    x_sib.append(remote(xwhole(2), xwhole(2), sib))
    zstep(4, 2)
    zstep(4, 3)
    lax.fori_loop(5, NZ - 1, prep, 0)
    u_local.wait()
    wg_local.wait()
    for d in u_y + w_y:
        d.wait_recv()

    same = (
        lax.broadcasted_iota(jnp.int32, (RP, RP), 0) // rank
        == lax.broadcasted_iota(jnp.int32, (RP, RP), 1) // rank
    )
    gram = jnp.where(same, mm(Ug[...], Ug[...], 0, 0), 0.0)
    kacc[...] = mm(Ug[...], Wg[...], 0, 0) + SCALE * mm(gram.astype(BF16), Db[...], 1, 0)
    for zz in range(NZ):
        pack(kS.at[zz], kacc[8 * zz : 8 * zz + 8, :].astype(BF16))
    k_z = [remote(kS.at[mod(z + j, NZ)], kR.at[z], at_z(j)) for j in range(1, NZ)]
    for d in x_sib:
        d.wait_recv()

    def scales(c):
        t0, t1, mask = trials_of(c)
        xc = X[c]
        dyc = dyA[c]
        q = jnp.where(mask, mm(xc, Ug[...], 1, 0), 0.0).astype(BF16)
        pre = mm(xc, Wg[...], 1, 0) + SCALE * mm(q, Db[...], 1, 0)
        e = dyc.astype(F32) * pre
        trow = lax.broadcasted_iota(jnp.int32, (8, qc), 0)
        s0 = jnp.sum(e[:hrow], axis=0, keepdims=True)
        s1 = jnp.sum(e[hrow:], axis=0, keepdims=True)
        dsS[...] += jnp.where(trow == t0, s0, 0.0) + jnp.where(trow == t1, s1, 0.0)
        qacc[...] += mm(q, dyc, 0, 0)

    def inputs(c):
        p = pA[c]
        xpT[...] += mm(p, X[c], 0, 0)
        dx = mm(gpA[c], Wg[...], 1, 1) + SCALE * mm(p, Ug[...], 1, 1)
        slot = lax.div(c, 2)

        @pl.when(lax.rem(c, 2) == k)
        def _():
            dxo[slot] = dx

        @pl.when(lax.rem(c, 2) != k)
        def _():
            dxs[slot] = dx.astype(BF16)
            pair_copy(slot).start()

    def pass_on(i):
        c = chunk_of(i)
        slot = lax.div(c, 2)

        @pl.when(lax.rem(c, 2) == k)
        def _():
            pair_copy(slot).wait_recv()
            total = dxo[slot] + pairR[slot].astype(F32)
            dxo[slot] = total

            @pl.when(slot != x)
            def _():
                xs[slot] = total[:hrow].astype(BF16)
                x_copy(slot, x).start()

            for yy in range(NY):
                yfS[slot, yy] = total[hrow:, yy * wd : (yy + 1) * wd].astype(BF16)
            for j in YJ:
                yf_copy(slot, j).start()

    def pass_twice(i):
        c = chunk_of(i)
        slot = lax.div(c, 2)

        @pl.when(lax.rem(c, 2) == k)
        def _():
            for j in YJ:
                yf_copy(slot, j).wait_recv()
            total = dxo[slot, hrow:, ywd]
            for j in (1, 2, 3):
                total = total + yfR[slot, mod(y + j, NY)].astype(F32)

            @pl.when(slot == x)
            def _():
                acc1[...] = total

            @pl.when(slot != x)
            def _():
                x2S[slot] = total.astype(BF16)
                x2_copy(slot, x).start()

    def step(i, carry):
        c = chunk_of(i)
        inputs(c)
        scales(c)

        @pl.when(i > 0)
        def _():
            pass_on(i - 1)

        @pl.when(i > 3)
        def _():
            pass_twice(i - 4)

        return carry

    lax.fori_loop(0, NZ - 1, step, 0)
    for key in ((1, 4, 0), (1, 4, 1), (-1, 4, 2), (-1, 4, 3)):
        ring[key].wait_recv()
    last = chunk_of(NZ - 1)
    scales(last)

    pack(dsP, dsS[0:trials, :])
    ds_z = [remote(dsP, dsR.at[z], at_z(j)) for j in range(1, NZ)]
    for zz in range(NZ):
        pack(qS.at[zz], qacc[8 * zz : 8 * zz + 8, :].astype(BF16))
    q_z = [remote(qS.at[mod(z + j, NZ)], qR.at[z], at_z(j)) for j in range(1, NZ)]
    prep(NZ - 1, 0)
    inputs(last)
    pass_on(NZ - 2)
    pass_twice(NZ - 5)
    pass_on(NZ - 1)
    for d in ds_z:
        d.wait_recv()
    dsum = dsP[...]
    for j in range(1, NZ):
        dsum = dsum + dsR[mod(z + j, NZ)]
    dsum = unpack(dsum, qc)
    pack(mgR.at[y], dsum / norm)
    mg_y = [remote(mgR.at[y], mgR.at[y], at_y(j)) for j in YJ]
    gf = -dsum * magq / (norm * norm * norm)
    gfS[0:trials, :] = gf
    dg = jnp.concatenate(
        [Dq[rank * t : rank * (t + 1), :] * gf[t : t + 1] for t in range(trials)]
        + [jnp.zeros((RP - tr, qc), F32)],
        axis=0,
    ).astype(BF16)
    inner = jnp.where(same, mm(dg, Db[...], 1, 1), 0.0).astype(BF16)
    up = SCALE * (xpT[...] + mm(dg, Wg[...], 1, 1) + SCALE * mm(inner, Ug[...], 1, 1))
    for yy in range(NY):
        upS[yy] = up[:tr, yy * wd : (yy + 1) * wd]
    up_y = [remote(upS.at[mod(y + j, NY)], upR.at[y], at_y(j)) for j in YJ]

    pass_twice(NZ - 4)
    pass_twice(NZ - 3)
    for d in k_z + q_z:
        d.wait_recv()
    zrows = pl.ds(pl.multiple_of(z * 8, 8), 8)
    qsum = qR[mod(z + 1, NZ)].astype(F32)
    ksum = kR[mod(z + 1, NZ)].astype(F32)
    for j in range(2, NZ):
        qsum = qsum + qR[mod(z + j, NZ)].astype(F32)
        ksum = ksum + kR[mod(z + j, NZ)].astype(F32)
    qsum = unpack(qsum, qc) + qacc[zrows, :]
    ksum = unpack(ksum, qc) + kacc[zrows, :]
    tz = lax.div(z * 8, rank)
    pack(
        dnY.at[y, z],
        (SCALE * (qsum * resS[pl.ds(tz, 1), :] + ksum * gfS[pl.ds(tz, 1), :])).astype(BF16),
    )
    dn_z = [remote(dnY.at[y, z], dnY.at[y, z], at_z(j)) for j in range(1, NZ)]

    pass_twice(NZ - 2)
    for d in up_y:
        d.wait_recv()
    upP[...] = upS[y] + upR[mod(y + 1, NY)] + upR[mod(y + 2, NY)] + upR[mod(y + 3, NY)]
    up_p = remote(upP, upPR, sib)

    pass_twice(NZ - 1)
    for d in dn_z:
        d.wait_recv()
    dn_y = [remote(dnY.at[y], dnY.at[y], at_y(j)) for j in YJ]

    up_p.wait_recv()
    upX[...] = upP[...] + upPR[...]
    up_x = [remote(upX, upXR.at[x], at_x(j)) for j in YJ]

    for j in (1, 2, 3):
        x_copy(mod(x + j, NX), mod(x + j, NX)).wait_recv()
    total = dxo[x, 0:hrow, :]
    for j in (1, 2, 3):
        total = total + xR[mod(x + j, NX)].astype(F32)
    dxo[x, 0:hrow, :] = total
    for yy in range(NY):
        ysS[yy] = total[:, yy * wd : (yy + 1) * wd].astype(BF16)
    ys_y = [remote(ysS.at[mod(y + j, NY)], ysR.at[y], at_y(j)) for j in YJ]

    for d in up_x:
        d.wait_recv()
    out_up[...] = upX[...] + upXR[mod(x + 1, NX)] + upXR[mod(x + 2, NX)] + upXR[mod(x + 3, NX)]
    for d in mg_y:
        d.wait_recv()
    out_mag[...] = mgR[...]
    for d in ys_y:
        d.wait_recv()
    acc = dxo[x, 0:hrow, ywd]
    for j in (1, 2, 3):
        acc = acc + ysR[mod(y + j, NY)].astype(F32)
    out_dx[0:hrow, :] = acc.astype(BF16)
    for j in (1, 2, 3):
        x2_copy(mod(x + j, NX), mod(x + j, NX)).wait_recv()
    acc = acc1[...]
    for j in (1, 2, 3):
        acc = acc + x2R[mod(x + j, NX)].astype(F32)
    out_dx[hrow:, :] = acc.astype(BF16)

    for d in dn_y:
        d.wait_recv()
    out_dn[...] = dnY[...]
    for d in sent:
        d.wait_send()
    for slot in range(NX):
        pair_copy(slot).wait_send()
        for j in YJ:
            yf_copy(slot, j).wait_send()
    for j in (1, 2, 3):
        x_copy(mod(x + j, NX), x).wait_send()
        x2_copy(mod(x + j, NX), x).wait_send()


def write_out(dx, mg, dnp, up, o_dx, o_mag, o_dn, o_up):
    o_dx[...] = dx[...]
    o_up[...] = up[...]
    trials, cols = o_mag.shape
    qc = cols // NY
    for yy in range(NY):
        o_mag[:, yy * qc : (yy + 1) * qc] = unpack(mg[yy], qc)
        for zz in range(NZ):
            o_dn[8 * zz : 8 * zz + 8, yy * qc : (yy + 1) * qc] = unpack(dnp[yy, zz].astype(F32), qc)


def local(acts, dy, w, down, up, mag, idx):
    trials, rank, cols = down.shape
    wd = w.shape[0]
    tok = acts.shape[0]
    qc = cols // NY
    tr = trials * rank
    dn = down.reshape(tr, cols)
    ut = jnp.transpose(up, (0, 2, 1)).reshape(tr, wd)
    V = pltpu.VMEM
    anyspec = pl.BlockSpec(memory_space=pl.ANY)
    vspec = pl.BlockSpec(memory_space=pltpu.VMEM)
    sspec = pl.BlockSpec(memory_space=pltpu.SMEM)
    width = NY * wd
    scratch = [
        V((NZ, tok, qc), BF16),
        V((2 * NX, tok, width), BF16),
        V((width, qc), BF16),
        V((wd, cols), BF16),
        V((width, RP), BF16),
        V((wd, RP), BF16),
        V((RP, wd), F32),
        V((RP, cols), F32),
        V((RP, qc), F32),
        V((RP, qc), BF16),
        V((NY, 8, HP), F32),
        V((NY, 8, HP), F32),
        V((8, HP), F32),
        V((NZ, 8, HP), F32),
        V((8, qc), F32),
        V((8, qc), F32),
        V((8, HP), F32),
        V((NZ, 8, HP), F32),
        V((8, qc), F32),
        V((RP, qc), F32),
        V((RP, qc), F32),
        V((RP, width), F32),
        V((NZ, 16, HP), BF16),
        V((NZ, 16, HP), BF16),
        V((NZ, 16, HP), BF16),
        V((NZ, 16, HP), BF16),
        V((NZ, tok, qc), BF16),
        V((NZ, tok, RP), BF16),
        V((NX, tok, width), F32),
        V((NX, tok, width), BF16),
        V((NX, tok, width), BF16),
        V((NX, tok // 2, width), BF16),
        V((NX, tok // 2, width), BF16),
        V((NY, tok // 2, wd), BF16),
        V((NY, tok // 2, wd), BF16),
        V((NX, NY, tok // 2, wd), BF16),
        V((NX, NY, tok // 2, wd), BF16),
        V((NX, tok // 2, wd), BF16),
        V((NX, tok // 2, wd), BF16),
        V((tok // 2, wd), F32),
        V((NY, tr, wd), F32),
        V((NY, tr, wd), F32),
        V((tr, wd), F32),
        V((tr, wd), F32),
        V((tr, wd), F32),
        V((NX, tr, wd), F32),
        V((NY, 8, HP), F32),
        V((NY, NZ, 16, HP), BF16),
        pltpu.SemaphoreType.DMA((112,)),
        pltpu.SemaphoreType.DMA((112,)),
        pltpu.SemaphoreType.DMA((16,)),
        pltpu.SemaphoreType.DMA((NX,)),
        pltpu.SemaphoreType.DMA((NX,)),
        pltpu.SemaphoreType.DMA((NX,)),
        pltpu.SemaphoreType.DMA((NX,)),
        pltpu.SemaphoreType.DMA((NX, 3)),
        pltpu.SemaphoreType.DMA((NX, 3)),
        pltpu.SemaphoreType.DMA((NX,)),
        pltpu.SemaphoreType.DMA((NX,)),
    ]
    dx, mg, dng, upg = pl.pallas_call(
        kernel,
        out_shape=(
            jax.ShapeDtypeStruct((tok, wd), BF16),
            jax.ShapeDtypeStruct((NY, 8, HP), F32),
            jax.ShapeDtypeStruct((NY, NZ, 16, HP), BF16),
            jax.ShapeDtypeStruct((tr, wd), F32),
        ),
        in_specs=[anyspec, anyspec, anyspec, anyspec, anyspec, vspec, sspec],
        out_specs=(vspec,) * 4,
        scratch_shapes=scratch,
        compiler_params=pltpu.CompilerParams(
            collective_id=0, has_side_effects=True, vmem_limit_bytes=56 * 1024 * 1024
        ),
        cost_estimate=pl.CostEstimate(flops=8_000_000_000, bytes_accessed=8_000_000, transcendentals=0),
    )(acts, dy, w, dn, ut, mag, idx)
    dx, mg, dng, upg = pl.pallas_call(
        write_out,
        out_shape=(
            jax.ShapeDtypeStruct((tok, wd), BF16),
            jax.ShapeDtypeStruct((trials, cols), F32),
            jax.ShapeDtypeStruct((tr, cols), F32),
            jax.ShapeDtypeStruct((tr, wd), F32),
        ),
        in_specs=[vspec] * 4,
        out_specs=(vspec,) * 4,
    )(dx, mg, dng, upg)
    return (
        dx,
        mg,
        dng.reshape(trials, rank, cols),
        jnp.transpose(upg.reshape(trials, rank, wd), (0, 2, 1)),
    )


def solution(mesh):
    in_specs = (
        P("col", "row"),
        P("row", "col"),
        P("row", "col"),
        P(None, None, "col"),
        P(None, "row", None),
        P(None, "col"),
        P(),
    )
    out_specs = (P("col", "row"), P(None, "col"), P(None, None, "col"), P(None, "row", None))
    return jax.shard_map(local, mesh=mesh, in_specs=in_specs, out_specs=out_specs, check_vma=False)
```

```python
import functools

import jax
import jax.numpy as jnp
from jax import lax
from jax.experimental import pallas as pl
from jax.experimental.pallas import tpu as pltpu
from jax.sharding import PartitionSpec as P

SCALE = 2.0
EPS = 1e-06
NX, NY, NZ = 4, 4, 8
MESH = pl.DeviceIdType.MESH
F32, BF16 = jnp.float32, jnp.bfloat16
HP = 512
RP = 128


def mm(a, b, ca, cb, precision=None):
    return lax.dot_general(
        a, b, (((ca,), (cb,)), ((), ())), precision=precision, preferred_element_type=F32
    )


def pack(ref, v):
    n = v.shape[0]
    ref[0:n, :] = v[:, :HP]
    ref[n : 2 * n, 0 : v.shape[1] - HP] = v[:, HP:]


def unpack(p, cols):
    n = p.shape[0] // 2
    return jnp.concatenate([p[:n], p[n:, : cols - HP]], axis=1)


def kernel(
    acts, dy, w, dn, ut, mag, idx,
    out_dx, out_mag, out_dn, out_up,
    dyA, X, Wg, Wo, Ug, Uo, UTs, Df, Dq, Db,
    nyS, nyR, nzS, nzR, resS,
    dsS, dsP, dsR, gfS, qacc, kacc, xpT, qS, qR, kS, kR,
    gpA, pA, dxo, dxs, pairR, xs, xR, ysS, ysR, yfS, yfR, x2S, x2R, acc1,
    upS, upR, upX, upXR, mgR, dnY,
    ss, rs, ls, ps, pr, xss, xrs, yfs, yfr, x2s, x2r,
):
    row, col = lax.axis_index("row"), lax.axis_index("col")
    z, y = lax.div(row, NY), lax.rem(row, NY)
    x, k = lax.div(col, 2), lax.rem(col, 2)
    rank = 16
    trials = 4
    rows = dy.shape[0]
    cols = w.shape[1]
    qc = cols // NY
    wd = w.shape[0]
    tok = acts.shape[0]
    tr = trials * rank
    hrow = tok // 2

    def mod(v, n):
        return lax.rem(v + n, n)

    def at_y(j):
        return (z * NY + mod(y + j, NY), col)

    def at_z(j):
        return (mod(z + j, NZ) * NY + y, col)

    def at_x(j):
        return (row, mod(x + j, NX) * 2 + k)

    sib = (row, x * 2 + 1 - k)
    YJ = (1, 3, 2)

    barrier = pltpu.get_barrier_semaphore()
    others = [(row, mod(x + j, NX) * 2 + 1 - k) for j in (1, 2, 3)]
    peers = [at_y(j) for j in YJ] + [at_x(j) for j in YJ] + [at_z(j) for j in range(1, NZ)]
    peers += others + [sib]
    for p in peers:
        pl.semaphore_signal(barrier, inc=1, device_id=p, device_id_type=MESH)

    count = [0, 0]
    sent = []

    def remote(src, dst, dev):
        i = count[0]
        count[0] += 1
        d = pltpu.make_async_remote_copy(
            src_ref=src, dst_ref=dst, send_sem=ss.at[i], recv_sem=rs.at[i],
            device_id=dev, device_id_type=MESH,
        )
        d.start()
        sent.append(d)
        return d

    def localcp(src, dst):
        i = count[1]
        count[1] += 1
        d = pltpu.make_async_copy(src, dst, ls.at[i])
        d.start()
        return d

    def yq(j):
        return pl.ds(pl.multiple_of(mod(y + j, NY) * qc, 128), qc)

    yrows = pl.ds(pl.multiple_of(y * rows, rows), rows)
    ywd = pl.ds(pl.multiple_of(y * wd, wd), wd)

    dy_local = localcp(dy.at[:, yq(0)], dyA.at[z, yrows, :])
    ut_local = localcp(ut, UTs.at[pl.ds(0, tr), :])
    wo_local = localcp(w, Wo)
    df_local = localcp(dn, Df.at[pl.ds(0, tr), :])
    act_local = localcp(acts, X.at[col, :, ywd])
    wg_local = localcp(w.at[:, yq(0)], Wg.at[ywd, :])
    UTs[tr:, :] = jnp.zeros((RP - tr, wd), F32)
    Df[tr:, :] = jnp.zeros((RP - tr, cols), F32)
    for ref in (dsS, qacc, xpT):
        ref[...] = jnp.zeros_like(ref)
    pl.semaphore_wait(barrier, len(peers))

    dy_y = [remote(dy.at[:, yq(j)], dyA.at[z, yrows, :], at_y(j)) for j in YJ]
    dy_local.wait()

    def chunk_of(i):
        s = lax.div(i + 1, 2)
        return lax.rem(z + s * (2 * lax.rem(i, 2) - 1) + NZ, NZ)

    def pair_copy(slot):
        return pltpu.make_async_remote_copy(
            src_ref=dxs.at[slot], dst_ref=pairR.at[slot], send_sem=ps.at[slot],
            recv_sem=pr.at[slot], device_id=sib, device_id_type=MESH,
        )

    def x_copy(to, frm):
        return pltpu.make_async_remote_copy(
            src_ref=xs.at[to], dst_ref=xR.at[frm], send_sem=xss.at[to],
            recv_sem=xrs.at[frm], device_id=(row, to * 2 + k), device_id_type=MESH,
        )

    def yf_copy(slot, j):
        return pltpu.make_async_remote_copy(
            src_ref=yfS.at[slot, mod(y + j, NY)], dst_ref=yfR.at[slot, y],
            send_sem=yfs.at[slot, j - 1], recv_sem=yfr.at[slot, j - 1],
            device_id=at_y(j), device_id_type=MESH,
        )

    def x2_copy(to, frm):
        return pltpu.make_async_remote_copy(
            src_ref=x2S.at[to], dst_ref=x2R.at[frm], send_sem=x2s.at[to],
            recv_sem=x2r.at[frm], device_id=(row, to * 2 + k), device_id_type=MESH,
        )

    def trials_of(c):
        t0, t1 = idx[2 * c], idx[2 * c + 1]
        sub = lax.broadcasted_iota(jnp.int32, (tok, RP), 0)
        lane = lax.broadcasted_iota(jnp.int32, (tok, RP), 1)
        return t0, t1, lane // rank == jnp.where(sub < hrow, t0, t1)

    def prep(i, carry):
        c = chunk_of(i)
        t0, t1, mask = trials_of(c)
        dyf = dyA[c].astype(F32)
        res = resS[0:trials, :]
        r0 = jnp.zeros((1, qc), F32)
        r1 = jnp.zeros((1, qc), F32)
        for t in range(trials):
            r0 = jnp.where(t0 == t, res[t : t + 1], r0)
            r1 = jnp.where(t1 == t, res[t : t + 1], r1)
        gpA[c, 0:hrow, :] = (dyf[:hrow] * r0).astype(BF16)
        gpA[c, hrow:, :] = (dyf[hrow:] * r1).astype(BF16)
        pA[c] = jnp.where(mask, mm(gpA[c], Db[...], 1, 1), 0.0).astype(BF16)
        return carry

    def kpart(yb):
        brows = pl.ds(pl.multiple_of(yb * wd, wd), wd)
        kacc[...] += mm(Ug[brows, :], Wg[brows, :], 0, 0)

    def scales(c):
        t0, t1, mask = trials_of(c)
        xc = X[c]
        dyc = dyA[c]
        q = jnp.where(mask, mm(xc, Ug[...], 1, 0), 0.0).astype(BF16)
        pre = mm(xc, Wg[...], 1, 0) + SCALE * mm(q, Db[...], 1, 0)
        e = dyc.astype(F32) * pre
        trow = lax.broadcasted_iota(jnp.int32, (8, qc), 0)
        s0 = jnp.sum(e[:hrow], axis=0, keepdims=True)
        s1 = jnp.sum(e[hrow:], axis=0, keepdims=True)
        dsS[...] += jnp.where(trow == t0, s0, 0.0) + jnp.where(trow == t1, s1, 0.0)
        qacc[...] += mm(q, dyc, 0, 0)

    def inputs(i, carry):
        c = chunk_of(i)
        xpT[...] += mm(pA[c], X[c], 0, 0)
        dx = mm(gpA[c], Wg[...], 1, 1) + SCALE * mm(pA[c], Ug[...], 1, 1)
        slot = lax.div(c, 2)

        @pl.when(lax.rem(c, 2) == k)
        def _():
            dxo[slot] = dx

        @pl.when(lax.rem(c, 2) != k)
        def _():
            dxs[slot] = dx.astype(BF16)
            pair_copy(slot).start()

        return carry

    def pass_on(i):
        c = chunk_of(i)
        slot = lax.div(c, 2)

        @pl.when(lax.rem(c, 2) == k)
        def _():
            pair_copy(slot).wait_recv()
            total = dxo[slot] + pairR[slot].astype(F32)
            dxo[slot] = total

            @pl.when(slot != x)
            def _():
                xs[slot] = total[:hrow].astype(BF16)
                x_copy(slot, x).start()

            for yy in range(NY):
                yfS[slot, yy] = total[hrow:, yy * wd : (yy + 1) * wd].astype(BF16)
            for j in YJ:
                yf_copy(slot, j).start()

    def pass_twice(i):
        c = chunk_of(i)
        slot = lax.div(c, 2)

        @pl.when(lax.rem(c, 2) == k)
        def _():
            for j in YJ:
                yf_copy(slot, j).wait_recv()
            total = dxo[slot, hrow:, ywd]
            for j in (1, 2, 3):
                total = total + yfR[slot, mod(y + j, NY)].astype(F32)

            @pl.when(slot == x)
            def _():
                acc1[...] = total

            @pl.when(slot != x)
            def _():
                x2S[slot] = total.astype(BF16)
                x2_copy(slot, x).start()

    ring = {}

    def zstep(step, b):
        ys = mod(y - (0, 1, 3, 2)[b], NY)
        brows = pl.ds(pl.multiple_of(ys * rows, rows), rows)
        for sign in (1, -1):
            if step > 1:
                ring[sign, step - 1, b].wait_recv()
            if step < 4 or (b < 2) == (sign == 1):
                src = dyA.at[mod(z - sign * (step - 1), NZ), brows, :]
                ring[sign, step, b] = remote(src, src, at_z(sign))

    zstep(1, 0)
    act_y = [remote(acts, X.at[col, :, ywd], at_y(j)) for j in YJ]
    ut_local.wait()
    Uo[...] = UTs[...].T.astype(BF16)
    u_local = localcp(Uo, Ug.at[ywd, :])
    df_local.wait()
    wo_local.wait()

    def norm_piece(yy):
        for h, (c0, n) in enumerate(((0, HP), (HP, qc - HP))):
            at = slice(yy * qc + c0, yy * qc + c0 + n)
            wb = Wo[:, at].astype(F32)
            db = (SCALE * Df[:, at]).astype(BF16)
            owner = lax.broadcasted_iota(jnp.int32, db.shape, 0) // rank
            for t in range(trials):
                m = wb + mm(Uo[...], jnp.where(owner == t, db, jnp.zeros_like(db)), 1, 0)
                r = h * trials + t
                nyS[yy, r : r + 1, 0:n] = jnp.sum(m * m, axis=0, keepdims=True)

    for yy in range(NY):
        norm_piece(yy)
    ny_y = [remote(nyS.at[mod(y + j, NY)], nyR.at[y], at_y(j)) for j in YJ]
    u_y = [remote(Uo, Ug.at[ywd, :], at_y(j)) for j in YJ]
    for b, d in enumerate(dy_y):
        d.wait_recv()
        zstep(1, b + 1)
    Dq[...] = Df[:, pl.ds(pl.multiple_of(y * qc, 128), qc)]
    Db[...] = Dq[...].astype(BF16)
    zstep(2, 0)
    for d in ny_y:
        d.wait_recv()
    nzS[...] = nyS[y] + nyR[mod(y + 1, NY)] + nyR[mod(y + 2, NY)] + nyR[mod(y + 3, NY)]
    nz_z = [remote(nzS, nzR.at[z], at_z(j)) for j in range(1, NZ)]
    zstep(2, 1)

    act_local.wait()
    for d in act_y:
        d.wait_recv()
    w_y = [remote(w.at[:, yq(j)], Wg.at[ywd, :], at_y(j)) for j in YJ]
    h0, h1 = pl.ds(0, hrow), pl.ds(hrow, hrow)

    def xpart(j, h):
        return X.at[mod(x + j, NX) * 2 + k, h, :]

    def xwhole(j):
        return X.at[mod(x + j, NX) * 2 + k]

    xp = [remote(xpart(0, h), xpart(0, h), at_x(1)) for h in (h0, h1)]
    xm = [remote(xpart(0, h), xpart(0, h), at_x(-1)) for h in (h1, h0)]
    x_sib = [remote(xwhole(0), xwhole(0), sib)]
    zstep(2, 2)
    zstep(2, 3)
    for d in nz_z:
        d.wait_recv()
    nsq = nzS[...]
    for j in range(1, NZ):
        nsq = nsq + nzR[mod(z + j, NZ)]
    norm = jnp.sqrt(unpack(nsq, qc) + EPS)
    magq = mag[:, pl.ds(pl.multiple_of(y * qc, 128), qc)]
    resS[0:trials, :] = magq / norm
    zstep(3, 0)

    u_local.wait()
    for d in u_y:
        d.wait_recv()
    same = (
        lax.broadcasted_iota(jnp.int32, (RP, RP), 0) // rank
        == lax.broadcasted_iota(jnp.int32, (RP, RP), 1) // rank
    )
    gram = jnp.where(same, mm(Ug[...], Ug[...], 0, 0), 0.0)
    kacc[...] = SCALE * mm(gram.astype(BF16), Db[...], 1, 0)
    wg_local.wait()
    kpart(y)
    lax.fori_loop(0, 3, prep, 0)
    zstep(3, 1)
    xp[0].wait_recv()
    xp.append(remote(xpart(-1, h0), xpart(-1, h0), at_x(1)))
    xm[0].wait_recv()
    xm.append(remote(xpart(1, h1), xpart(1, h1), at_x(-1)))
    zstep(3, 2)
    zstep(3, 3)
    xp[1].wait_recv()
    xm[1].wait_recv()
    x_sib += [remote(xwhole(j), xwhole(j), sib) for j in (-1, 1)]
    zstep(4, 0)
    lax.fori_loop(3, 5, prep, 0)
    zstep(4, 1)
    xp[2].wait_recv()
    xm[2].wait_recv()
    x_sib.append(remote(xwhole(2), xwhole(2), sib))
    zstep(4, 2)
    for j, d in zip((1, 3), w_y):
        d.wait_recv()
        kpart(mod(y - j, NY))
    zstep(4, 3)
    lax.fori_loop(5, NZ - 1, prep, 0)
    w_y[2].wait_recv()
    kpart(mod(y - 2, NY))
    for zz in range(NZ):
        pack(kS.at[zz], kacc[8 * zz : 8 * zz + 8, :].astype(BF16))
    k_z = [remote(kS.at[mod(z + j, NZ)], kR.at[z], at_z(j)) for j in range(1, NZ)]
    for d in x_sib:
        d.wait_recv()

    def step(i, carry):
        inputs(i, carry)
        scales(chunk_of(i))

        @pl.when(i > 0)
        def _():
            pass_on(i - 1)

        @pl.when(i > 3)
        def _():
            pass_twice(i - 4)

        return carry

    lax.fori_loop(0, NZ - 1, step, 0)
    for key in ((1, 4, 0), (1, 4, 1), (-1, 4, 2), (-1, 4, 3)):
        ring[key].wait_recv()
    last = chunk_of(NZ - 1)
    scales(last)
    pack(dsP, dsS[0:trials, :])
    ds_z = [remote(dsP, dsR.at[z], at_z(j)) for j in range(1, NZ)]
    for zz in range(NZ):
        pack(qS.at[zz], qacc[8 * zz : 8 * zz + 8, :].astype(BF16))
    q_z = [remote(qS.at[mod(z + j, NZ)], qR.at[z], at_z(j)) for j in range(1, NZ)]

    prep(NZ - 1, 0)
    inputs(NZ - 1, 0)
    pass_on(NZ - 2)
    pass_twice(NZ - 5)
    pass_twice(NZ - 4)
    pass_on(NZ - 1)
    for d in ds_z:
        d.wait_recv()
    dsum = dsP[...]
    for j in range(1, NZ):
        dsum = dsum + dsR[mod(z + j, NZ)]
    dsum = unpack(dsum, qc)
    gf = -dsum * magq / (norm * norm * norm)
    gfS[0:trials, :] = gf
    for d in k_z + q_z:
        d.wait_recv()
    zrows = pl.ds(pl.multiple_of(z * 8, 8), 8)
    qsum = qR[mod(z + 1, NZ)].astype(F32)
    ksum = kR[mod(z + 1, NZ)].astype(F32)
    for j in range(2, NZ):
        qsum = qsum + qR[mod(z + j, NZ)].astype(F32)
        ksum = ksum + kR[mod(z + j, NZ)].astype(F32)
    qsum = unpack(qsum, qc) + qacc[zrows, :]
    ksum = unpack(ksum, qc) + kacc[zrows, :]
    tz = lax.div(z * 8, rank)
    pack(
        dnY.at[y, z],
        (SCALE * (qsum * resS[pl.ds(tz, 1), :] + ksum * gfS[pl.ds(tz, 1), :])).astype(BF16),
    )
    ZJ = (1, 7, 2, 6, 3, 5, 4)
    dn_z = [remote(dnY.at[y, z], dnY.at[y, z], at_z(j)) for j in ZJ]
    dn_y = [remote(dnY.at[y, z], dnY.at[y, z], at_y(j)) for j in YJ]
    dg = jnp.concatenate(
        [Dq[rank * t : rank * (t + 1), :] * gf[t : t + 1] for t in range(trials)]
        + [jnp.zeros((RP - tr, qc), F32)],
        axis=0,
    ).astype(BF16)
    inner = jnp.where(same, mm(dg, Db[...], 1, 1), 0.0).astype(BF16)
    up = SCALE * (xpT[...] + mm(dg, Wg[...], 1, 1) + SCALE * mm(inner, Ug[...], 1, 1))
    xpT[...] = up
    for yy in range(NY):
        upS[yy] = up[:tr, yy * wd : (yy + 1) * wd].astype(BF16)
    up_y = [remote(upS.at[mod(y + j, NY)], upR.at[y], at_y(j)) for j in YJ]
    pack(mgR.at[y], dsum / norm)
    mg_y = [remote(mgR.at[y], mgR.at[y], at_y(j)) for j in YJ]
    pass_twice(NZ - 3)
    pass_twice(NZ - 2)
    for d in up_y:
        d.wait_recv()
    upP = xpT[0:tr, ywd]
    for j in (1, 2, 3):
        upP = upP + upR[mod(y + j, NY)].astype(F32)
    upX[...] = upP.astype(BF16)
    up_x = [remote(upX, upXR.at[col], dev) for dev in [at_x(j) for j in YJ] + others + [sib]]
    for j, d in zip(ZJ, dn_z):
        d.wait_recv()
        piece = dnY.at[y, mod(z - j, NZ)]
        dn_y += [remote(piece, piece, at_y(i)) for i in YJ]
    pass_twice(NZ - 1)

    for j in (1, 2, 3):
        x_copy(mod(x + j, NX), mod(x + j, NX)).wait_recv()
    total = dxo[x, 0:hrow, :]
    for j in (1, 2, 3):
        total = total + xR[mod(x + j, NX)].astype(F32)
    dxo[x, 0:hrow, :] = total
    for yy in range(NY):
        ysS[yy] = total[:, yy * wd : (yy + 1) * wd].astype(BF16)
    ys_y = [remote(ysS.at[mod(y + j, NY)], ysR.at[y], at_y(j)) for j in YJ]

    for d in up_x:
        d.wait_recv()
    for j in range(1, 2 * NX):
        upP = upP + upXR[mod(col + j, 2 * NX)].astype(F32)
    out_up[...] = upP
    for d in mg_y:
        d.wait_recv()
    out_mag[...] = mgR[...]
    for d in ys_y:
        d.wait_recv()
    acc = dxo[x, 0:hrow, ywd]
    for j in (1, 2, 3):
        acc = acc + ysR[mod(y + j, NY)].astype(F32)
    out_dx[0:hrow, :] = acc.astype(BF16)
    for j in (1, 2, 3):
        x2_copy(mod(x + j, NX), mod(x + j, NX)).wait_recv()
    acc = acc1[...]
    for j in (1, 2, 3):
        acc = acc + x2R[mod(x + j, NX)].astype(F32)
    out_dx[hrow:, :] = acc.astype(BF16)

    for d in dn_y:
        d.wait_recv()
    out_dn[...] = dnY[...]
    for d in sent:
        d.wait_send()
    for slot in range(NX):
        pair_copy(slot).wait_send()
        for j in YJ:
            yf_copy(slot, j).wait_send()
    for j in (1, 2, 3):
        x_copy(mod(x + j, NX), x).wait_send()
        x2_copy(mod(x + j, NX), x).wait_send()


def write_out(dx, mg, dnp, up, o_dx, o_mag, o_dn, o_up):
    o_dx[...] = dx[...]
    o_up[...] = up[...]
    trials, cols = o_mag.shape
    qc = cols // NY
    for yy in range(NY):
        o_mag[:, yy * qc : (yy + 1) * qc] = unpack(mg[yy], qc)
        for zz in range(NZ):
            o_dn[8 * zz : 8 * zz + 8, yy * qc : (yy + 1) * qc] = unpack(dnp[yy, zz].astype(F32), qc)


def local(acts, dy, w, down, up, mag, idx):
    trials, rank, cols = down.shape
    wd = w.shape[0]
    tok = acts.shape[0]
    qc = cols // NY
    tr = trials * rank
    dn = down.reshape(tr, cols)
    ut = jnp.transpose(up, (0, 2, 1)).reshape(tr, wd)
    V = pltpu.VMEM
    anyspec = pl.BlockSpec(memory_space=pl.ANY)
    vspec = pl.BlockSpec(memory_space=pltpu.VMEM)
    sspec = pl.BlockSpec(memory_space=pltpu.SMEM)
    width = NY * wd
    scratch = [
        V((NZ, tok, qc), BF16),
        V((2 * NX, tok, width), BF16),
        V((width, qc), BF16),
        V((wd, cols), BF16),
        V((width, RP), BF16),
        V((wd, RP), BF16),
        V((RP, wd), F32),
        V((RP, cols), F32),
        V((RP, qc), F32),
        V((RP, qc), BF16),
        V((NY, 8, HP), F32),
        V((NY, 8, HP), F32),
        V((8, HP), F32),
        V((NZ, 8, HP), F32),
        V((8, qc), F32),
        V((8, qc), F32),
        V((8, HP), F32),
        V((NZ, 8, HP), F32),
        V((8, qc), F32),
        V((RP, qc), F32),
        V((RP, qc), F32),
        V((RP, width), F32),
        V((NZ, 16, HP), BF16),
        V((NZ, 16, HP), BF16),
        V((NZ, 16, HP), BF16),
        V((NZ, 16, HP), BF16),
        V((NZ, tok, qc), BF16),
        V((NZ, tok, RP), BF16),
        V((NX, tok, width), F32),
        V((NX, tok, width), BF16),
        V((NX, tok, width), BF16),
        V((NX, tok // 2, width), BF16),
        V((NX, tok // 2, width), BF16),
        V((NY, tok // 2, wd), BF16),
        V((NY, tok // 2, wd), BF16),
        V((NX, NY, tok // 2, wd), BF16),
        V((NX, NY, tok // 2, wd), BF16),
        V((NX, tok // 2, wd), BF16),
        V((NX, tok // 2, wd), BF16),
        V((tok // 2, wd), F32),
        V((NY, tr, wd), BF16),
        V((NY, tr, wd), BF16),
        V((tr, wd), BF16),
        V((2 * NX, tr, wd), BF16),
        V((NY, 8, HP), F32),
        V((NY, NZ, 16, HP), BF16),
        pltpu.SemaphoreType.DMA((144,)),
        pltpu.SemaphoreType.DMA((144,)),
        pltpu.SemaphoreType.DMA((16,)),
        pltpu.SemaphoreType.DMA((NX,)),
        pltpu.SemaphoreType.DMA((NX,)),
        pltpu.SemaphoreType.DMA((NX,)),
        pltpu.SemaphoreType.DMA((NX,)),
        pltpu.SemaphoreType.DMA((NX, 3)),
        pltpu.SemaphoreType.DMA((NX, 3)),
        pltpu.SemaphoreType.DMA((NX,)),
        pltpu.SemaphoreType.DMA((NX,)),
    ]
    dx, mg, dng, upg = pl.pallas_call(
        kernel,
        out_shape=(
            jax.ShapeDtypeStruct((tok, wd), BF16),
            jax.ShapeDtypeStruct((NY, 8, HP), F32),
            jax.ShapeDtypeStruct((NY, NZ, 16, HP), BF16),
            jax.ShapeDtypeStruct((tr, wd), F32),
        ),
        in_specs=[anyspec, anyspec, anyspec, anyspec, anyspec, vspec, sspec],
        out_specs=(vspec,) * 4,
        scratch_shapes=scratch,
        compiler_params=pltpu.CompilerParams(
            collective_id=0, has_side_effects=True, vmem_limit_bytes=56 * 1024 * 1024
        ),
        cost_estimate=pl.CostEstimate(flops=8_000_000_000, bytes_accessed=8_000_000, transcendentals=0),
    )(acts, dy, w, dn, ut, mag, idx)
    dx, mg, dng, upg = pl.pallas_call(
        write_out,
        out_shape=(
            jax.ShapeDtypeStruct((tok, wd), BF16),
            jax.ShapeDtypeStruct((trials, cols), F32),
            jax.ShapeDtypeStruct((tr, cols), F32),
            jax.ShapeDtypeStruct((tr, wd), F32),
        ),
        in_specs=[vspec] * 4,
        out_specs=(vspec,) * 4,
    )(dx, mg, dng, upg)
    return (
        dx,
        mg,
        dng.reshape(trials, rank, cols),
        jnp.transpose(upg.reshape(trials, rank, wd), (0, 2, 1)),
    )


def solution(mesh):
    in_specs = (
        P("col", "row"),
        P("row", "col"),
        P("row", "col"),
        P(None, None, "col"),
        P(None, "row", None),
        P(None, "col"),
        P(),
    )
    out_specs = (P("col", "row"), P(None, "col"), P(None, None, "col"), P(None, "row", None))
    return jax.shard_map(local, mesh=mesh, in_specs=in_specs, out_specs=out_specs, check_vma=False)
```

```python
import functools

import jax
import jax.numpy as jnp
from jax import lax
from jax.experimental import pallas as pl
from jax.experimental.pallas import tpu as pltpu
from jax.sharding import PartitionSpec as P

SCALE = 2.0
SPLIT = 96
EPS = 1e-06
NX, NY, NZ = 4, 4, 8
MESH = pl.DeviceIdType.MESH
F32, BF16 = jnp.float32, jnp.bfloat16
HP = 512
RP = 128


def mm(a, b, ca, cb, precision=None):
    return lax.dot_general(
        a, b, (((ca,), (cb,)), ((), ())), precision=precision, preferred_element_type=F32
    )


def pack(ref, v):
    n = v.shape[0]
    ref[0:n, :] = v[:, :HP]
    ref[n : 2 * n, 0 : v.shape[1] - HP] = v[:, HP:]


def unpack(p, cols):
    n = p.shape[0] // 2
    return jnp.concatenate([p[:n], p[n:, : cols - HP]], axis=1)


def kernel(
    acts, dy, w, dn, ut, mag, idx,
    out_dx, out_mag, out_dn, out_up,
    dyA, X, Wg, Wo, Ug, Uo, UTs, Df, Dq, Db,
    nyS, nyR, nzS, nzR, resS,
    dsS, dsP, dsR, gfS, qacc, kacc, xpT, qS, qR, kS, kR,
    gpA, pA, dxo, dxs, pairR, xs, xR, ysS, ysR, yfS, yfR, x2S, x2R, acc1,
    upS, upR, upX, upXR, mgR, dnY,
    ss, rs, ls, ps, pr, xss, xrs, yfs, yfr, x2s, x2r,
):
    row, col = lax.axis_index("row"), lax.axis_index("col")
    z, y = lax.div(row, NY), lax.rem(row, NY)
    x, k = lax.div(col, 2), lax.rem(col, 2)
    rank = 16
    trials = 4
    rows = dy.shape[0]
    cols = w.shape[1]
    qc = cols // NY
    wd = w.shape[0]
    tok = acts.shape[0]
    tr = trials * rank
    hrow = tok // 2

    def mod(v, n):
        return lax.rem(v + n, n)

    def at_y(j):
        return (z * NY + mod(y + j, NY), col)

    def at_z(j):
        return (mod(z + j, NZ) * NY + y, col)

    def at_x(j):
        return (row, mod(x + j, NX) * 2 + k)

    sib = (row, x * 2 + 1 - k)
    YJ = (1, 3, 2)

    barrier = pltpu.get_barrier_semaphore()
    others = [(row, mod(x + j, NX) * 2 + 1 - k) for j in (1, 2, 3)]
    peers = [at_y(j) for j in YJ] + [at_x(j) for j in YJ] + [at_z(j) for j in range(1, NZ)]
    peers += others + [sib]
    for p in peers:
        pl.semaphore_signal(barrier, inc=1, device_id=p, device_id_type=MESH)

    count = [0, 0]
    sent = []

    def remote(src, dst, dev):
        i = count[0]
        count[0] += 1
        d = pltpu.make_async_remote_copy(
            src_ref=src, dst_ref=dst, send_sem=ss.at[i], recv_sem=rs.at[i],
            device_id=dev, device_id_type=MESH,
        )
        d.start()
        sent.append(d)
        return d

    def localcp(src, dst):
        i = count[1]
        count[1] += 1
        d = pltpu.make_async_copy(src, dst, ls.at[i])
        d.start()
        return d

    def yq(j):
        return pl.ds(pl.multiple_of(mod(y + j, NY) * qc, 128), qc)

    yrows = pl.ds(pl.multiple_of(y * rows, rows), rows)
    ywd = pl.ds(pl.multiple_of(y * wd, wd), wd)

    dy_local = localcp(dy.at[:, yq(0)], dyA.at[z, yrows, :])
    ut_local = localcp(ut, UTs.at[pl.ds(0, tr), :])
    wo_local = localcp(w, Wo)
    df_local = localcp(dn, Df.at[pl.ds(0, tr), :])
    act_local = localcp(acts, X.at[col, :, ywd])
    wg_local = localcp(w.at[:, yq(0)], Wg.at[ywd, :])
    UTs[tr:, :] = jnp.zeros((RP - tr, wd), F32)
    Df[tr:, :] = jnp.zeros((RP - tr, cols), F32)
    for ref in (dsS, qacc, xpT):
        ref[...] = jnp.zeros_like(ref)
    pl.semaphore_wait(barrier, len(peers))

    dy_y = [remote(dy.at[:, yq(j)], dyA.at[z, yrows, :], at_y(j)) for j in YJ]
    dy_local.wait()

    def chunk_of(i):
        s = lax.div(i + 1, 2)
        return lax.rem(z + s * (2 * lax.rem(i, 2) - 1) + NZ, NZ)

    def pair_copy(slot):
        return pltpu.make_async_remote_copy(
            src_ref=dxs.at[slot], dst_ref=pairR.at[slot], send_sem=ps.at[slot],
            recv_sem=pr.at[slot], device_id=sib, device_id_type=MESH,
        )

    def x_copy(to, frm):
        return pltpu.make_async_remote_copy(
            src_ref=xs.at[to], dst_ref=xR.at[frm], send_sem=xss.at[to],
            recv_sem=xrs.at[frm], device_id=(row, to * 2 + k), device_id_type=MESH,
        )

    def yf_copy(slot, j):
        return pltpu.make_async_remote_copy(
            src_ref=yfS.at[slot, mod(y + j, NY)], dst_ref=yfR.at[slot, y],
            send_sem=yfs.at[slot, j - 1], recv_sem=yfr.at[slot, j - 1],
            device_id=at_y(j), device_id_type=MESH,
        )

    def x2_copy(to, frm):
        return pltpu.make_async_remote_copy(
            src_ref=x2S.at[to], dst_ref=x2R.at[frm], send_sem=x2s.at[to],
            recv_sem=x2r.at[frm], device_id=(row, to * 2 + k), device_id_type=MESH,
        )

    def trials_of(c):
        t0, t1 = idx[2 * c], idx[2 * c + 1]
        sub = lax.broadcasted_iota(jnp.int32, (tok, RP), 0)
        lane = lax.broadcasted_iota(jnp.int32, (tok, RP), 1)
        return t0, t1, lane // rank == jnp.where(sub < hrow, t0, t1)

    def prep(i, carry):
        c = chunk_of(i)
        t0, t1, mask = trials_of(c)
        dyf = dyA[c].astype(F32)
        res = resS[0:trials, :]
        r0 = jnp.zeros((1, qc), F32)
        r1 = jnp.zeros((1, qc), F32)
        for t in range(trials):
            r0 = jnp.where(t0 == t, res[t : t + 1], r0)
            r1 = jnp.where(t1 == t, res[t : t + 1], r1)
        gpA[c, 0:hrow, :] = (dyf[:hrow] * r0).astype(BF16)
        gpA[c, hrow:, :] = (dyf[hrow:] * r1).astype(BF16)
        pA[c] = jnp.where(mask, mm(gpA[c], Db[...], 1, 1), 0.0).astype(BF16)
        return carry

    def kpart(yb):
        brows = pl.ds(pl.multiple_of(yb * wd, wd), wd)
        kacc[...] += mm(Ug[brows, :], Wg[brows, :], 0, 0)

    def scales(c):
        t0, t1, mask = trials_of(c)
        xc = X[c]
        dyc = dyA[c]
        q = jnp.where(mask, mm(xc, Ug[...], 1, 0), 0.0).astype(BF16)
        pre = mm(xc, Wg[...], 1, 0) + SCALE * mm(q, Db[...], 1, 0)
        e = dyc.astype(F32) * pre
        trow = lax.broadcasted_iota(jnp.int32, (8, qc), 0)
        s0 = jnp.sum(e[:hrow], axis=0, keepdims=True)
        s1 = jnp.sum(e[hrow:], axis=0, keepdims=True)
        dsS[...] += jnp.where(trow == t0, s0, 0.0) + jnp.where(trow == t1, s1, 0.0)
        qacc[...] += mm(q, dyc, 0, 0)

    def inputs(i, carry):
        c = chunk_of(i)
        xpT[...] += mm(pA[c], X[c], 0, 0)
        dx = mm(gpA[c], Wg[...], 1, 1) + SCALE * mm(pA[c], Ug[...], 1, 1)
        slot = lax.div(c, 2)

        @pl.when(lax.rem(c, 2) == k)
        def _():
            dxo[slot] = dx

        @pl.when(lax.rem(c, 2) != k)
        def _():
            dxs[slot] = dx.astype(BF16)
            pair_copy(slot).start()

        return carry

    def pass_on(i):
        c = chunk_of(i)
        slot = lax.div(c, 2)

        @pl.when(lax.rem(c, 2) == k)
        def _():
            pair_copy(slot).wait_recv()
            total = dxo[slot] + pairR[slot].astype(F32)
            dxo[slot] = total

            @pl.when(slot != x)
            def _():
                xs[slot] = total[:SPLIT].astype(BF16)
                x_copy(slot, x).start()

            for yy in range(NY):
                yfS[slot, yy] = total[SPLIT:, yy * wd : (yy + 1) * wd].astype(BF16)
            for j in YJ:
                yf_copy(slot, j).start()

    def pass_twice(i):
        c = chunk_of(i)
        slot = lax.div(c, 2)

        @pl.when(lax.rem(c, 2) == k)
        def _():
            for j in YJ:
                yf_copy(slot, j).wait_recv()
            total = dxo[slot, SPLIT:, ywd]
            for j in (1, 2, 3):
                total = total + yfR[slot, mod(y + j, NY)].astype(F32)

            @pl.when(slot == x)
            def _():
                acc1[...] = total

            @pl.when(slot != x)
            def _():
                x2S[slot] = total.astype(BF16)
                x2_copy(slot, x).start()

    ring = {}

    def zstep(step, b):
        ys = mod(y - (0, 1, 3, 2)[b], NY)
        brows = pl.ds(pl.multiple_of(ys * rows, rows), rows)
        for sign in (1, -1):
            if step > 1:
                ring[sign, step - 1, b].wait_recv()
            if step < 4 or (b < 2) == (sign == 1):
                src = dyA.at[mod(z - sign * (step - 1), NZ), brows, :]
                ring[sign, step, b] = remote(src, src, at_z(sign))

    zstep(1, 0)
    act_y = [remote(acts, X.at[col, :, ywd], at_y(j)) for j in YJ]
    ut_local.wait()
    Uo[...] = UTs[...].T.astype(BF16)
    u_local = localcp(Uo, Ug.at[ywd, :])
    df_local.wait()
    wo_local.wait()

    def norm_piece(yy):
        for h, (c0, n) in enumerate(((0, HP), (HP, qc - HP))):
            at = slice(yy * qc + c0, yy * qc + c0 + n)
            wb = Wo[:, at].astype(F32)
            db = (SCALE * Df[:, at]).astype(BF16)
            owner = lax.broadcasted_iota(jnp.int32, db.shape, 0) // rank
            for t in range(trials):
                m = wb + mm(Uo[...], jnp.where(owner == t, db, jnp.zeros_like(db)), 1, 0)
                r = h * trials + t
                nyS[yy, r : r + 1, 0:n] = jnp.sum(m * m, axis=0, keepdims=True)

    for yy in range(NY):
        norm_piece(yy)
    ny_y = [remote(nyS.at[mod(y + j, NY)], nyR.at[y], at_y(j)) for j in YJ]
    u_y = [remote(Uo, Ug.at[ywd, :], at_y(j)) for j in YJ]
    for b, d in enumerate(dy_y):
        d.wait_recv()
        zstep(1, b + 1)
    Dq[...] = Df[:, pl.ds(pl.multiple_of(y * qc, 128), qc)]
    Db[...] = Dq[...].astype(BF16)
    zstep(2, 0)
    for d in ny_y:
        d.wait_recv()
    nzS[...] = nyS[y] + nyR[mod(y + 1, NY)] + nyR[mod(y + 2, NY)] + nyR[mod(y + 3, NY)]
    nz_z = [remote(nzS, nzR.at[z], at_z(j)) for j in range(1, NZ)]
    zstep(2, 1)

    act_local.wait()
    for d in act_y:
        d.wait_recv()
    w_y = [remote(w.at[:, yq(j)], Wg.at[ywd, :], at_y(j)) for j in YJ]
    h0, h1 = pl.ds(0, hrow), pl.ds(hrow, hrow)

    def xpart(j, h):
        return X.at[mod(x + j, NX) * 2 + k, h, :]

    def xwhole(j):
        return X.at[mod(x + j, NX) * 2 + k]

    xp = [remote(xpart(0, h), xpart(0, h), at_x(1)) for h in (h0, h1)]
    xm = [remote(xpart(0, h), xpart(0, h), at_x(-1)) for h in (h1, h0)]
    x_sib = [remote(xwhole(0), xwhole(0), sib)]
    zstep(2, 2)
    zstep(2, 3)
    for d in nz_z:
        d.wait_recv()
    nsq = nzS[...]
    for j in range(1, NZ):
        nsq = nsq + nzR[mod(z + j, NZ)]
    norm = jnp.sqrt(unpack(nsq, qc) + EPS)
    magq = mag[:, pl.ds(pl.multiple_of(y * qc, 128), qc)]
    resS[0:trials, :] = magq / norm
    zstep(3, 0)

    u_local.wait()
    for d in u_y:
        d.wait_recv()
    same = (
        lax.broadcasted_iota(jnp.int32, (RP, RP), 0) // rank
        == lax.broadcasted_iota(jnp.int32, (RP, RP), 1) // rank
    )
    gram = jnp.where(same, mm(Ug[...], Ug[...], 0, 0), 0.0)
    kacc[...] = SCALE * mm(gram.astype(BF16), Db[...], 1, 0)
    wg_local.wait()
    kpart(y)
    lax.fori_loop(0, 3, prep, 0)
    zstep(3, 1)
    xp[0].wait_recv()
    xp.append(remote(xpart(-1, h0), xpart(-1, h0), at_x(1)))
    xm[0].wait_recv()
    xm.append(remote(xpart(1, h1), xpart(1, h1), at_x(-1)))
    zstep(3, 2)
    zstep(3, 3)
    xp[1].wait_recv()
    xm[1].wait_recv()
    x_sib += [remote(xwhole(j), xwhole(j), sib) for j in (-1, 1)]
    zstep(4, 0)
    lax.fori_loop(3, 5, prep, 0)
    zstep(4, 1)
    xp[2].wait_recv()
    xm[2].wait_recv()
    x_sib.append(remote(xwhole(2), xwhole(2), sib))
    zstep(4, 2)
    for j, d in zip((1, 3), w_y):
        d.wait_recv()
        kpart(mod(y - j, NY))
    zstep(4, 3)
    lax.fori_loop(5, NZ - 1, prep, 0)
    w_y[2].wait_recv()
    kpart(mod(y - 2, NY))
    for zz in range(NZ):
        pack(kS.at[zz], kacc[8 * zz : 8 * zz + 8, :].astype(BF16))
    k_z = [remote(kS.at[mod(z + j, NZ)], kR.at[z], at_z(j)) for j in range(1, NZ)]
    for d in x_sib:
        d.wait_recv()

    def step(i, carry):
        inputs(i, carry)
        scales(chunk_of(i))

        @pl.when(i > 0)
        def _():
            pass_on(i - 1)

        @pl.when(i > 3)
        def _():
            pass_twice(i - 4)

        return carry

    lax.fori_loop(0, NZ - 1, step, 0)
    for key in ((1, 4, 0), (1, 4, 1), (-1, 4, 2), (-1, 4, 3)):
        ring[key].wait_recv()
    last = chunk_of(NZ - 1)
    scales(last)
    pack(dsP, dsS[0:trials, :])
    ds_z = [remote(dsP, dsR.at[z], at_z(j)) for j in range(1, NZ)]
    for zz in range(NZ):
        pack(qS.at[zz], qacc[8 * zz : 8 * zz + 8, :].astype(BF16))
    q_z = [remote(qS.at[mod(z + j, NZ)], qR.at[z], at_z(j)) for j in range(1, NZ)]

    prep(NZ - 1, 0)
    inputs(NZ - 1, 0)
    pass_on(NZ - 2)
    pass_twice(NZ - 5)
    pass_twice(NZ - 4)
    pass_on(NZ - 1)
    for d in ds_z:
        d.wait_recv()
    dsum = dsP[...]
    for j in range(1, NZ):
        dsum = dsum + dsR[mod(z + j, NZ)]
    dsum = unpack(dsum, qc)
    gf = -dsum * magq / (norm * norm * norm)
    gfS[0:trials, :] = gf
    for d in k_z + q_z:
        d.wait_recv()
    zrows = pl.ds(pl.multiple_of(z * 8, 8), 8)
    qsum = qR[mod(z + 1, NZ)].astype(F32)
    ksum = kR[mod(z + 1, NZ)].astype(F32)
    for j in range(2, NZ):
        qsum = qsum + qR[mod(z + j, NZ)].astype(F32)
        ksum = ksum + kR[mod(z + j, NZ)].astype(F32)
    qsum = unpack(qsum, qc) + qacc[zrows, :]
    ksum = unpack(ksum, qc) + kacc[zrows, :]
    tz = lax.div(z * 8, rank)
    pack(
        dnY.at[y, z],
        (SCALE * (qsum * resS[pl.ds(tz, 1), :] + ksum * gfS[pl.ds(tz, 1), :])).astype(BF16),
    )
    ZJ = (1, 7, 2, 6, 3, 5, 4)
    dn_z = [remote(dnY.at[y, z], dnY.at[y, z], at_z(j)) for j in ZJ]
    dn_y = [remote(dnY.at[y, z], dnY.at[y, z], at_y(j)) for j in YJ]
    dg = jnp.concatenate(
        [Dq[rank * t : rank * (t + 1), :] * gf[t : t + 1] for t in range(trials)]
        + [jnp.zeros((RP - tr, qc), F32)],
        axis=0,
    ).astype(BF16)
    inner = jnp.where(same, mm(dg, Db[...], 1, 1), 0.0).astype(BF16)
    up = SCALE * (xpT[...] + mm(dg, Wg[...], 1, 1) + SCALE * mm(inner, Ug[...], 1, 1))
    xpT[...] = up
    for yy in range(NY):
        upS[yy] = up[:tr, yy * wd : (yy + 1) * wd].astype(BF16)
    up_y = [remote(upS.at[mod(y + j, NY)], upR.at[y], at_y(j)) for j in YJ]
    pack(mgR.at[y], dsum / norm)
    mg_y = [remote(mgR.at[y], mgR.at[y], at_y(j)) for j in YJ]
    pass_twice(NZ - 3)
    pass_twice(NZ - 2)
    for d in up_y:
        d.wait_recv()
    upP = xpT[0:tr, ywd]
    for j in (1, 2, 3):
        upP = upP + upR[mod(y + j, NY)].astype(F32)
    upX[...] = upP.astype(BF16)
    up_x = [remote(upX, upXR.at[col], dev) for dev in [at_x(j) for j in YJ] + others + [sib]]
    for j, d in zip(ZJ, dn_z):
        d.wait_recv()
        piece = dnY.at[y, mod(z - j, NZ)]
        dn_y += [remote(piece, piece, at_y(i)) for i in YJ]
    pass_twice(NZ - 1)

    for j in (1, 2, 3):
        x_copy(mod(x + j, NX), mod(x + j, NX)).wait_recv()
    total = dxo[x, 0:SPLIT, :]
    for j in (1, 2, 3):
        total = total + xR[mod(x + j, NX)].astype(F32)
    dxo[x, 0:SPLIT, :] = total
    for yy in range(NY):
        ysS[yy] = total[:, yy * wd : (yy + 1) * wd].astype(BF16)
    ys_y = [remote(ysS.at[mod(y + j, NY)], ysR.at[y], at_y(j)) for j in YJ]

    for d in up_x:
        d.wait_recv()
    for j in range(1, 2 * NX):
        upP = upP + upXR[mod(col + j, 2 * NX)].astype(F32)
    out_up[...] = upP
    for d in mg_y:
        d.wait_recv()
    out_mag[...] = mgR[...]
    for d in ys_y:
        d.wait_recv()
    acc = dxo[x, 0:SPLIT, ywd]
    for j in (1, 2, 3):
        acc = acc + ysR[mod(y + j, NY)].astype(F32)
    out_dx[0:SPLIT, :] = acc.astype(BF16)
    for j in (1, 2, 3):
        x2_copy(mod(x + j, NX), mod(x + j, NX)).wait_recv()
    acc = acc1[...]
    for j in (1, 2, 3):
        acc = acc + x2R[mod(x + j, NX)].astype(F32)
    out_dx[SPLIT:, :] = acc.astype(BF16)

    for d in dn_y:
        d.wait_recv()
    out_dn[...] = dnY[...]
    for d in sent:
        d.wait_send()
    for slot in range(NX):
        pair_copy(slot).wait_send()
        for j in YJ:
            yf_copy(slot, j).wait_send()
    for j in (1, 2, 3):
        x_copy(mod(x + j, NX), x).wait_send()
        x2_copy(mod(x + j, NX), x).wait_send()


def write_out(dx, mg, dnp, up, o_dx, o_mag, o_dn, o_up):
    o_dx[...] = dx[...]
    o_up[...] = up[...]
    trials, cols = o_mag.shape
    qc = cols // NY
    for yy in range(NY):
        o_mag[:, yy * qc : (yy + 1) * qc] = unpack(mg[yy], qc)
        for zz in range(NZ):
            o_dn[8 * zz : 8 * zz + 8, yy * qc : (yy + 1) * qc] = unpack(dnp[yy, zz].astype(F32), qc)


def local(acts, dy, w, down, up, mag, idx):
    trials, rank, cols = down.shape
    wd = w.shape[0]
    tok = acts.shape[0]
    qc = cols // NY
    tr = trials * rank
    dn = down.reshape(tr, cols)
    ut = jnp.transpose(up, (0, 2, 1)).reshape(tr, wd)
    V = pltpu.VMEM
    anyspec = pl.BlockSpec(memory_space=pl.ANY)
    vspec = pl.BlockSpec(memory_space=pltpu.VMEM)
    sspec = pl.BlockSpec(memory_space=pltpu.SMEM)
    width = NY * wd
    scratch = [
        V((NZ, tok, qc), BF16),
        V((2 * NX, tok, width), BF16),
        V((width, qc), BF16),
        V((wd, cols), BF16),
        V((width, RP), BF16),
        V((wd, RP), BF16),
        V((RP, wd), F32),
        V((RP, cols), F32),
        V((RP, qc), F32),
        V((RP, qc), BF16),
        V((NY, 8, HP), F32),
        V((NY, 8, HP), F32),
        V((8, HP), F32),
        V((NZ, 8, HP), F32),
        V((8, qc), F32),
        V((8, qc), F32),
        V((8, HP), F32),
        V((NZ, 8, HP), F32),
        V((8, qc), F32),
        V((RP, qc), F32),
        V((RP, qc), F32),
        V((RP, width), F32),
        V((NZ, 16, HP), BF16),
        V((NZ, 16, HP), BF16),
        V((NZ, 16, HP), BF16),
        V((NZ, 16, HP), BF16),
        V((NZ, tok, qc), BF16),
        V((NZ, tok, RP), BF16),
        V((NX, tok, width), F32),
        V((NX, tok, width), BF16),
        V((NX, tok, width), BF16),
        V((NX, SPLIT, width), BF16),
        V((NX, SPLIT, width), BF16),
        V((NY, SPLIT, wd), BF16),
        V((NY, SPLIT, wd), BF16),
        V((NX, NY, tok - SPLIT, wd), BF16),
        V((NX, NY, tok - SPLIT, wd), BF16),
        V((NX, tok - SPLIT, wd), BF16),
        V((NX, tok - SPLIT, wd), BF16),
        V((tok - SPLIT, wd), F32),
        V((NY, tr, wd), BF16),
        V((NY, tr, wd), BF16),
        V((tr, wd), BF16),
        V((2 * NX, tr, wd), BF16),
        V((NY, 8, HP), F32),
        V((NY, NZ, 16, HP), BF16),
        pltpu.SemaphoreType.DMA((144,)),
        pltpu.SemaphoreType.DMA((144,)),
        pltpu.SemaphoreType.DMA((16,)),
        pltpu.SemaphoreType.DMA((NX,)),
        pltpu.SemaphoreType.DMA((NX,)),
        pltpu.SemaphoreType.DMA((NX,)),
        pltpu.SemaphoreType.DMA((NX,)),
        pltpu.SemaphoreType.DMA((NX, 3)),
        pltpu.SemaphoreType.DMA((NX, 3)),
        pltpu.SemaphoreType.DMA((NX,)),
        pltpu.SemaphoreType.DMA((NX,)),
    ]
    dx, mg, dng, upg = pl.pallas_call(
        kernel,
        out_shape=(
            jax.ShapeDtypeStruct((tok, wd), BF16),
            jax.ShapeDtypeStruct((NY, 8, HP), F32),
            jax.ShapeDtypeStruct((NY, NZ, 16, HP), BF16),
            jax.ShapeDtypeStruct((tr, wd), F32),
        ),
        in_specs=[anyspec, anyspec, anyspec, anyspec, anyspec, vspec, sspec],
        out_specs=(vspec,) * 4,
        scratch_shapes=scratch,
        compiler_params=pltpu.CompilerParams(
            collective_id=0, has_side_effects=True, vmem_limit_bytes=56 * 1024 * 1024
        ),
        cost_estimate=pl.CostEstimate(flops=8_000_000_000, bytes_accessed=8_000_000, transcendentals=0),
    )(acts, dy, w, dn, ut, mag, idx)
    dx, mg, dng, upg = pl.pallas_call(
        write_out,
        out_shape=(
            jax.ShapeDtypeStruct((tok, wd), BF16),
            jax.ShapeDtypeStruct((trials, cols), F32),
            jax.ShapeDtypeStruct((tr, cols), F32),
            jax.ShapeDtypeStruct((tr, wd), F32),
        ),
        in_specs=[vspec] * 4,
        out_specs=(vspec,) * 4,
    )(dx, mg, dng, upg)
    return (
        dx,
        mg,
        dng.reshape(trials, rank, cols),
        jnp.transpose(upg.reshape(trials, rank, wd), (0, 2, 1)),
    )


def solution(mesh):
    in_specs = (
        P("col", "row"),
        P("row", "col"),
        P("row", "col"),
        P(None, None, "col"),
        P(None, "row", None),
        P(None, "col"),
        P(),
    )
    out_specs = (P("col", "row"), P(None, "col"), P(None, None, "col"), P(None, "row", None))
    return jax.shard_map(local, mesh=mesh, in_specs=in_specs, out_specs=out_specs, check_vma=False)
```
